512 devices in a mesh: band: 32 (over z, y_hi), domain: 16 (over x, y_lo, core).
Axes of the slice: x: 4, y: 8 (y_hi: 4, y_lo: 2; y = y_hi * 2 + y_lo), z: 8, core: 2. Of those that a mesh axis runs over, the one named last changes fastest.
Arguments:
- orbitals: float32 [64, 16, 16, 16, 128], P('band', 'domain'), may hold values from -24 to 24
- potential: float32 [16, 16, 16, 128], P('domain'), may hold values from 0 to 1.5
Outputs:
- filtered: float32 [64, 16, 16, 16, 128], P('band', 'domain')
- intersection: float32 [64, 64], P('band')
- projected: float32 [64, 64], P('band')
The draws below stay inside these ranges and needn't reach their ends.
All inputs are finite; a program needn't handle non-finite values.
Results may differ from the reference program's by a relative error of at most 0.00005.
Values sent between devices are 32-bit elements; how exact they have to be, the bound alone decides.
A program may use at most 128 MiB of HBM per device.

```python
import jax
import jax.numpy as jnp
from jax import lax

CX = 16
CY = 16
CZ = 128
NB = 64
NX = 64
NY = 32
NZ = 256
NCELL = 524288
N_DOMAIN = 16


def draw_orbitals(key, part):
    key = jax.random.fold_in(key, 11)
    key_noise, key_fields, key_mix = jax.random.split(key, 3)
    shape = (NB, N_DOMAIN, CX, CY, CZ)
    field_shape = (8, N_DOMAIN, CX, CY, CZ)
    noise = jax.random.normal(key_noise, shape, jnp.float32)
    fields = jax.random.normal(key_fields, field_shape, jnp.float32)
    mixing = 0.4 * jax.random.normal(key_mix, (NB, 8), jnp.float32)
    total = noise
    for which in range(8):
        total = total + mixing[:, which][:, None, None, None, None] * fields[which][None]
    total = jnp.clip(total, -8.0, 8.0)
    block_x = jnp.arange(N_DOMAIN) // 4
    cell_x = jnp.arange(CX)
    position = (block_x[:, None] * CX + cell_x[None, :]).astype(jnp.float32)
    profile = jnp.exp(jnp.log(3.0) * position / float(max(NX - 1, 1)))
    return total * profile[None, :, :, None, None]


def steps_of(own_key, dims, cuts, low, largest):
    def one(dim, blocks):
        heights = jax.random.uniform(jax.random.fold_in(jax.random.fold_in(own_key, 6), dim), (blocks,), jnp.float32, low / len(cuts), largest / len(cuts))
        return jnp.repeat(jnp.exp(heights), dims[dim] // blocks).reshape((-1,) + (1,) * (len(dims) - dim - 1))

    gain = one(*cuts[0])
    for cut in cuts[1:]:
        gain = gain * one(*cut)
    return gain


def setup_inputs(seed: int = 0) -> dict:
    key_of = jax.random.split(jax.random.key(seed), 3)
    orbitals = draw_orbitals(jax.random.fold_in(key_of[2], 71), 0)
    potential = jnp.clip(1.5 * jax.random.uniform(key_of[1], (N_DOMAIN, CX, CY, CZ), jnp.float32) ** steps_of(key_of[1], (N_DOMAIN, CX, CY, CZ), ((0, 16),), -0.2, 0.2), 0.0, 1.5)
    return {"orbitals": orbitals, "potential": potential}


second_coeffs = (-5369.0 / 1800.0, 12.0 / 7.0, -15.0 / 56.0, 10.0 / 189.0, -1.0 / 112.0, 2.0 / 1925.0, -1.0 / 16632.0)
filter_center = 6.5
filter_half = 5.5


def second_roll(values, axis):
    total = second_coeffs[0] * values
    for step in range(1, 7):
        total = total + second_coeffs[step] * (jnp.roll(values, -step, axis) + jnp.roll(values, step, axis))
    return total


def to_grid(block):
    count_x = NX // CX
    shaped = block.reshape(count_x, 2, 2, CX, CY, CZ).transpose(0, 3, 1, 4, 2, 5)
    return shaped.reshape(NX, NY, NZ)


def from_grid(grid):
    count_x = NX // CX
    shaped = grid.reshape(count_x, CX, 2, CY, 2, CZ).transpose(0, 2, 4, 1, 3, 5)
    return shaped.reshape(count_x * 4, CX, CY, CZ)


def reference(orbitals, potential):
    grid_pot = to_grid(potential)

    def hamiltonian(values):
        lap = second_roll(values, 0) + second_roll(values, 1) + second_roll(values, 2)
        return -0.5 * lap + grid_pot * values

    def one_band(block):
        start = to_grid(block)
        first = (hamiltonian(start) - filter_center * start) / filter_half
        second = 2.0 * (hamiltonian(first) - filter_center * first) / filter_half - start
        applied = hamiltonian(second)
        return from_grid(second), from_grid(applied)

    filtered, applied = lax.map(one_band, orbitals)
    flat = filtered.reshape(NB, -1)
    hflat = applied.reshape(NB, -1)
    intersection = jnp.dot(flat, flat.T, precision=lax.Precision.HIGHEST, preferred_element_type=jnp.float32) / float(NCELL)
    projected = jnp.dot(hflat, flat.T, precision=lax.Precision.HIGHEST, preferred_element_type=jnp.float32) / float(NCELL)
    return filtered, intersection, projected
```

```python
import functools

import jax
import jax.numpy as jnp
from jax import lax
from jax.experimental import pallas as pl
from jax.experimental.pallas import tpu as pltpu
from jax.sharding import PartitionSpec as P

second_coeffs = (
    -5369.0 / 1800.0,
    12.0 / 7.0,
    -15.0 / 56.0,
    10.0 / 189.0,
    -1.0 / 112.0,
    2.0 / 1925.0,
    -1.0 / 16632.0,
)
filter_center = 6.5
filter_half = 5.5
reach = 6
MESH = pl.DeviceIdType.MESH

CX, CY, CZ = 16, 16, 128
NY = 32
NB = 64
NCELL = 524288


def hamiltonian(src, j, beside, pot, lane):
    here = src[j]
    total = (-1.5 * second_coeffs[0] + pot) * here
    for s in range(1, reach + 1):
        pair = src[j + s] + src[j - s]
        pair = pair + (pltpu.roll(here, s, 0) + pltpu.roll(here, NY - s, 0))
        ahead = pltpu.roll(jnp.where(lane < s, beside, here), CZ - s, 1)
        behind = pltpu.roll(jnp.where(lane >= CZ - s, beside, here), s, 1)
        total = total + (-0.5 * second_coeffs[s]) * (pair + (ahead + behind))
    return total


def kernel(
    orb_in, pot_in, out_f, out_s, out_p,
    orb, pot, first, fil, zo, zf, zs, hf, gf, gh, part, r1, r2, tot,
    loc_sem, in_send, in_recv, core_send, core_recv, x_send, x_recv,
    a2a_send, a2a_recv, back_send, back_recv, red_send, red_recv,
):
    band = lax.axis_index("band")
    domain = lax.axis_index("domain")
    z, yh = band // 4, band % 4
    x, yl, core = domain // 4, (domain // 2) % 2, domain % 2
    y = yh * 2 + yl
    zy = z * 8 + y
    mine = pl.multiple_of(yl * CY, CY)
    other = pl.multiple_of((1 - yl) * CY, CY)

    def at(pz, py, px, pc):
        return (pz * 4 + py // 2, px * 4 + (py % 2) * 2 + pc)

    xn, xp = (x + 1) % 4, (x + 3) % 4
    yo = y + 1 - 2 * yl
    yq = (y + 7 + 2 * yl) % 8
    mate = at(z, y, x, 1 - core)

    def rdma(src, dst, send, recv, to):
        return pltpu.make_async_remote_copy(
            src_ref=src, dst_ref=dst, send_sem=send, recv_sem=recv,
            device_id=to, device_id_type=MESH,
        )

    local = [
        pltpu.make_async_copy(orb_in.at[yl], orb.at[pl.ds(12, CX), pl.ds(mine, CY)], loc_sem.at[0]),
        pltpu.make_async_copy(pot_in, pot.at[pl.ds(6, CX), pl.ds(mine, CY)], loc_sem.at[1]),
    ]
    for c in local:
        c.start()

    bar = pltpu.get_barrier_semaphore()

    def hello(to):
        pl.semaphore_signal(bar, inc=1, device_id=to, device_id_type=MESH)

    for px in (xn, xp):
        hello(at(z, yo, px, core))
        hello(at(z, yq, px, core))

    def hello_near(j, _):
        hello(((z * 4 + (yh ^ (j >> 3))), (x ^ ((j >> 1) & 3)) * 4 + yl * 2 + (core ^ (j & 1))))
        return 0

    def hello_plane(j, _):
        a, kz = j >> 3, j & 7
        hello(at(z ^ kz, y ^ (a ^ kz), x, core))
        return 0

    lax.fori_loop(1, 2, hello_near, 0)
    lax.fori_loop(2, 8, hello_near, 0)
    for k in (1, 2, 3):
        lax.fori_loop(k * 8 + 1, k * 8 + 8, hello_near, 0)
    lax.fori_loop(1, 64, hello_plane, 0)
    pl.semaphore_wait(bar, 4 + 28 + 63)

    rows = pl.ds(mine, CY)
    entry = [
        rdma(orb_in.at[1 - yl], orb.at[pl.ds(12, CX), rows], in_send.at[0], in_recv.at[0], at(z, yo, x, core)),
        rdma(orb_in.at[1 - yl, pl.ds(4, 12)], orb.at[pl.ds(0, 12), rows], in_send.at[1], in_recv.at[1], at(z, yo, xn, core)),
        rdma(orb_in.at[1 - yl, pl.ds(0, 12)], orb.at[pl.ds(28, 12), rows], in_send.at[2], in_recv.at[2], at(z, yo, xp, core)),
        rdma(orb_in.at[yl, pl.ds(4, 12)], orb.at[pl.ds(0, 12), rows], in_send.at[3], in_recv.at[3], at(z, y, xn, core)),
        rdma(orb_in.at[yl, pl.ds(0, 12)], orb.at[pl.ds(28, 12), rows], in_send.at[4], in_recv.at[4], at(z, y, xp, core)),
        rdma(pot_in, pot.at[pl.ds(6, CX), rows], in_send.at[5], in_recv.at[5], at(z, yq, x, core)),
        rdma(pot_in.at[pl.ds(10, 6)], pot.at[pl.ds(0, 6), rows], in_send.at[6], in_recv.at[6], at(z, yq, xn, core)),
        rdma(pot_in.at[pl.ds(0, 6)], pot.at[pl.ds(22, 6), rows], in_send.at[7], in_recv.at[7], at(z, yq, xp, core)),
        rdma(pot_in.at[pl.ds(10, 6)], pot.at[pl.ds(0, 6), rows], in_send.at[8], in_recv.at[8], at(z, y, xn, core)),
        rdma(pot_in.at[pl.ds(0, 6)], pot.at[pl.ds(22, 6), rows], in_send.at[9], in_recv.at[9], at(z, y, xp, core)),
    ]
    for c in entry:
        c.start()
    for c in local:
        c.wait()

    def to_mate(k, src, dst):
        c = rdma(src, dst, core_send.at[k], core_recv.at[k], mate)
        c.start()
        return c

    beside = [to_mate(0, orb.at[pl.ds(12, CX), pl.ds(mine, CY)], zo.at[pl.ds(6, CX), pl.ds(mine, CY)])]
    entry[0].wait_recv()
    beside.append(to_mate(1, orb.at[pl.ds(12, CX), pl.ds(other, CY)], zo.at[pl.ds(6, CX), pl.ds(other, CY)]))
    entry[1].wait_recv()
    entry[3].wait_recv()
    beside.append(to_mate(2, orb.at[pl.ds(6, 6)], zo.at[pl.ds(0, 6)]))
    entry[2].wait_recv()
    entry[4].wait_recv()
    beside.append(to_mate(3, orb.at[pl.ds(28, 6)], zo.at[pl.ds(22, 6)]))
    for c in entry[5:]:
        c.wait_recv()
    for c in beside:
        c.wait_recv()

    lane = lax.broadcasted_iota(jnp.int32, (NY, CZ), 1)

    def step_first(k, _):
        h = hamiltonian(orb, k + 6, zo[k], pot[k] - filter_center, lane)
        first[k] = h * (1.0 / filter_half)
        return 0

    lax.fori_loop(0, CX + 12, step_first, 0)

    mid = pl.ds(6, CX)
    beside.append(to_mate(4, first.at[mid], zf))
    beside[4].wait_recv()

    def step_filtered(k, _):
        h = hamiltonian(first, k + 6, zf[k], pot[k + 6] - filter_center, lane)
        fil[k + 6] = h * (2.0 / filter_half) - orb[k + 12]
        return 0

    lax.fori_loop(0, CX, step_filtered, 0)

    rims = [
        rdma(fil.at[pl.ds(6, 6)], fil.at[pl.ds(22, 6)], x_send.at[0], x_recv.at[0], at(z, y, xp, core)),
        rdma(fil.at[pl.ds(16, 6)], fil.at[pl.ds(0, 6)], x_send.at[1], x_recv.at[1], at(z, y, xn, core)),
    ]
    for c in rims:
        c.start()
    beside.append(to_mate(5, fil.at[mid], zs))

    def spread(src, low, got, which):
        def send(j, _):
            a, kz = j >> 3, j & 7
            pz, py = z ^ kz, y ^ (a ^ kz)
            row = pl.multiple_of((py % 4) * 8, 8)
            rdma(
                src.at[low + pz * 2 + py // 4, pl.ds(row, 8)], got.at[zy],
                a2a_send.at[which], a2a_recv.at[which], at(pz, py, x, core),
            ).start()
            return 0

        lax.fori_loop(1, 64, send, 0)
        got[zy] = src[low + zy // 4, pl.ds(pl.multiple_of((zy % 4) * 8, 8), 8)]

    def spread_all(got, which):
        return rdma(got.at[pl.ds(0, 63)], got.at[pl.ds(0, 63)], a2a_send.at[which], a2a_recv.at[which], mate)

    spread(fil, 6, gf, 0)

    for c in rims:
        c.wait_recv()
    beside[5].wait_recv()

    def step_applied(k, _):
        hf[k] = hamiltonian(fil, k + 6, zs[k], pot[k + 6], lane)
        return 0

    lax.fori_loop(0, CX, step_applied, 0)
    spread(hf, 0, gh, 1)

    back = rdma(fil.at[mid, pl.ds(other, CY)], out_f.at[yl], back_send, back_recv, at(z, yo, x, core))
    back.start()
    keep = pltpu.make_async_copy(fil.at[mid, pl.ds(mine, CY)], out_f.at[yl], loc_sem.at[2])
    keep.start()

    def contract(left, right):
        return lax.dot_general(
            left, right, (((1,), (1,)), ((), ())),
            precision=lax.Precision.HIGHEST, preferred_element_type=jnp.float32,
        )

    spread_all(gf, 0).wait_recv()
    spread_all(gh, 1).wait_recv()
    both = jnp.zeros((NB, 2 * NB), jnp.float32)
    for s in range(8):
        left = gf[:, s, :]
        both = both + contract(left, jnp.concatenate([left, gh[:, s, :]], axis=0))
    part[...] = both.reshape(8, 8, 2 * NB)

    slot = z * 2 + yl

    def send_rows(j, _):
        pz, pl_ = z ^ (j >> 1), yl ^ (j & 1)
        rdma(
            part.at[pz], r1.at[slot], red_send.at[0], red_recv.at[0],
            (pz * 4 + yh, x * 4 + pl_ * 2 + core),
        ).start()
        return 0

    lax.fori_loop(1, 16, send_rows, 0)
    r1[slot] = part[z]
    red1 = rdma(r1.at[pl.ds(0, 15)], r1.at[pl.ds(0, 15)], red_send.at[0], red_recv.at[0], mate)
    red1.wait_recv()
    tot[...] = jnp.sum(r1[...], axis=0)

    slot2 = yh * 8 + x * 2 + core

    def send_total(j, _):
        rdma(
            tot, r2.at[slot2], red_send.at[1], red_recv.at[1],
            (z * 4 + (yh ^ (j >> 3)), (x ^ ((j >> 1) & 3)) * 4 + yl * 2 + (core ^ (j & 1))),
        ).start()
        return 0

    lax.fori_loop(1, 32, send_total, 0)
    r2[slot2] = tot[...]
    red2 = rdma(r2.at[pl.ds(0, 31)], r2.at[pl.ds(0, 31)], red_send.at[1], red_recv.at[1], mate)
    red2.wait_recv()
    r1[0] = jnp.sum(r2[...], axis=0) * (1.0 / NCELL)
    rows = r1[0, pl.ds(yh * 2, 2), :]
    out_s[...] = rows[:, :NB]
    out_p[...] = rows[:, NB:]

    for c in entry:
        c.wait_send()
    for c in beside:
        c.wait_send()
    for c in rims:
        c.wait_send()
    spread_all(gf, 0).wait_send()
    spread_all(gh, 1).wait_send()
    red1.wait_send()
    red2.wait_send()
    keep.wait()
    back.wait()


def shards(orbitals, potential):
    f32 = jnp.float32
    vmem = pltpu.VMEM
    dma = pltpu.SemaphoreType.DMA
    any_ = pl.BlockSpec(memory_space=pl.ANY)
    full = pl.BlockSpec(memory_space=pltpu.VMEM)
    filtered, inter, proj = pl.pallas_call(
        kernel,
        out_shape=(
            jax.ShapeDtypeStruct((2, CX, CY, CZ), f32),
            jax.ShapeDtypeStruct((2, NB), f32),
            jax.ShapeDtypeStruct((2, NB), f32),
        ),
        in_specs=[any_, any_],
        out_specs=(any_, full, full),
        scratch_shapes=[
            vmem((CX + 24, NY, CZ), f32),
            vmem((CX + 12, NY, CZ), f32),
            vmem((CX + 12, NY, CZ), f32),
            vmem((CX + 12, NY, CZ), f32),
            vmem((CX + 12, NY, CZ), f32),
            vmem((CX, NY, CZ), f32),
            vmem((CX, NY, CZ), f32),
            vmem((CX, NY, CZ), f32),
            vmem((NB, 8, CZ), f32),
            vmem((NB, 8, CZ), f32),
            vmem((8, 8, 2 * NB), f32),
            vmem((16, 8, 2 * NB), f32),
            vmem((32, 8, 2 * NB), f32),
            vmem((8, 2 * NB), f32),
            dma((3,)), dma((10,)), dma((10,)), dma((6,)), dma((6,)), dma((2,)), dma((2,)),
            dma((2,)), dma((2,)), dma, dma, dma((2,)), dma((2,)),
        ],
        compiler_params=pltpu.CompilerParams(
            collective_id=0, has_side_effects=True, vmem_limit_bytes=32 << 20
        ),
        name="chebyshev_step",
    )(orbitals.reshape(2, CX, CY, CZ), potential.reshape(CX, CY, CZ))
    return filtered[:, None], inter, proj


def solution(mesh):
    return jax.shard_map(
        shards,
        mesh=mesh,
        in_specs=(P("band", "domain", None, None, None), P("domain", None, None, None)),
        out_specs=(P("band", "domain", None, None, None), P("band", None), P("band", None)),
        check_vma=False,
    )
```

```python
import functools

import jax
import jax.numpy as jnp
from jax import lax
from jax.experimental import pallas as pl
from jax.experimental.pallas import tpu as pltpu
from jax.sharding import PartitionSpec as P

second_coeffs = (
    -5369.0 / 1800.0,
    12.0 / 7.0,
    -15.0 / 56.0,
    10.0 / 189.0,
    -1.0 / 112.0,
    2.0 / 1925.0,
    -1.0 / 16632.0,
)
filter_center = 6.5
filter_half = 5.5
reach = 6
MESH = pl.DeviceIdType.MESH

CX, CY, CZ = 16, 16, 128
NY = 32
NB = 64
NCELL = 524288


def part_y(here, pot):
    total = (-1.5 * second_coeffs[0] + pot) * here
    for s in range(1, reach + 1):
        pair = pltpu.roll(here, s, 0) + pltpu.roll(here, NY - s, 0)
        total = total + (-0.5 * second_coeffs[s]) * pair
    return total


def part_z(here, beside, lane):
    total = None
    for s in range(1, reach + 1):
        ahead = pltpu.roll(jnp.where(lane < s, beside, here), CZ - s, 1)
        behind = pltpu.roll(jnp.where(lane >= CZ - s, beside, here), s, 1)
        term = (-0.5 * second_coeffs[s]) * (ahead + behind)
        total = term if total is None else total + term
    return total


def part_x(src, j):
    total = None
    for s in range(1, reach + 1):
        term = (-0.5 * second_coeffs[s]) * (src[j + s] + src[j - s])
        total = term if total is None else total + term
    return total


def far_first(i, half):
    return half + ((i + 1) // 2) * (2 * (i % 2) - 1)


def kernel(
    orb_in, pot_in, out_f, out_s, out_p,
    orb, pot, first, fil, zo, zf, zs, acc, hf, gf, gh, part, r1, r2, tot,
    loc_sem, in_send, in_recv, core_send, core_recv, x_send, x_recv,
    a2a_send, a2a_recv, back_send, back_recv, red_send, red_recv,
):
    band = lax.axis_index("band")
    domain = lax.axis_index("domain")
    z, yh = band // 4, band % 4
    x, yl, core = domain // 4, (domain // 2) % 2, domain % 2
    y = yh * 2 + yl
    zy = z * 8 + y
    mine = pl.multiple_of(yl * CY, CY)
    other = pl.multiple_of((1 - yl) * CY, CY)

    def at(pz, py, px, pc):
        return (pz * 4 + py // 2, px * 4 + (py % 2) * 2 + pc)

    xn, xp = (x + 1) % 4, (x + 3) % 4
    yo = y + 1 - 2 * yl
    yq = (y + 7 + 2 * yl) % 8
    mate = at(z, y, x, 1 - core)
    to_xn, to_xp = at(z, y, xn, core), at(z, y, xp, core)

    def rdma(src, dst, send, recv, to):
        return pltpu.make_async_remote_copy(
            src_ref=src, dst_ref=dst, send_sem=send, recv_sem=recv,
            device_id=to, device_id_type=MESH,
        )

    mid = pl.ds(6, CX)
    low, high = pl.ds(0, 6), pl.ds(22, 6)
    rows = pl.ds(mine, CY)
    rows_other = pl.ds(other, CY)

    local = [
        pltpu.make_async_copy(orb_in.at[yl], orb.at[mid, rows], loc_sem.at[0]),
        pltpu.make_async_copy(pot_in, pot.at[:, rows], loc_sem.at[1]),
    ]
    for c in local:
        c.start()

    bar = pltpu.get_barrier_semaphore()

    def hello(to):
        pl.semaphore_signal(bar, inc=1, device_id=to, device_id_type=MESH)

    hello(at(z, yo, xn, core))
    hello(at(z, yo, xp, core))

    def hello_near(j, _):
        hello(((z * 4 + (yh ^ (j >> 3))), (x ^ ((j >> 1) & 3)) * 4 + yl * 2 + (core ^ (j & 1))))
        return 0

    def hello_plane(j, _):
        a, kz = j >> 3, j & 7
        hello(at(z ^ kz, y ^ (a ^ kz), x, core))
        return 0

    lax.fori_loop(1, 8, hello_near, 0)
    for k in (1, 2, 3):
        lax.fori_loop(k * 8 + 1, k * 8 + 8, hello_near, 0)
    lax.fori_loop(1, 64, hello_plane, 0)
    pl.semaphore_wait(bar, 2 + 28 + 63)

    entry = [
        rdma(orb_in.at[1 - yl], orb.at[mid, rows], in_send.at[0], in_recv.at[0], at(z, yo, x, core)),
        rdma(orb_in.at[1 - yl, pl.ds(10, 6)], orb.at[low, rows], in_send.at[1], in_recv.at[1], at(z, yo, xn, core)),
        rdma(orb_in.at[1 - yl, pl.ds(0, 6)], orb.at[high, rows], in_send.at[2], in_recv.at[2], at(z, yo, xp, core)),
        rdma(orb_in.at[yl, pl.ds(10, 6)], orb.at[low, rows], in_send.at[3], in_recv.at[3], to_xn),
        rdma(orb_in.at[yl, pl.ds(0, 6)], orb.at[high, rows], in_send.at[4], in_recv.at[4], to_xp),
        rdma(pot_in, pot.at[:, rows], in_send.at[5], in_recv.at[5], at(z, yq, x, core)),
    ]

    def to_mate(k, src, dst):
        c = rdma(src, dst, core_send.at[k], core_recv.at[k], mate)
        c.start()
        return c

    beside = [to_mate(0, orb_in.at[yl], zo.at[:, rows])]
    for c in entry:
        c.start()
    for c in local:
        c.wait()
    entry[0].wait_recv()
    beside.append(to_mate(1, orb.at[mid, rows_other], zo.at[:, rows_other]))
    entry[5].wait_recv()

    lane = lax.broadcasted_iota(jnp.int32, (NY, CZ), 1)

    def over_layers(body):
        def step(k, _):
            body(k)
            return 0

        lax.fori_loop(0, CX, step, 0)

    def along_y(src):
        def body(k):
            acc[k] = part_y(src[k + 6], pot[k])

        return body

    def along_z(src, beside_src):
        def body(k):
            acc[k] = acc[k] + part_z(src[k + 6], beside_src[k], lane)

        return body

    def rims_of(src, k):
        cs = [
            rdma(src.at[pl.ds(6, 6)], src.at[high], x_send.at[k], x_recv.at[k], to_xp),
            rdma(src.at[pl.ds(16, 6)], src.at[low], x_send.at[k + 1], x_recv.at[k + 1], to_xn),
        ]
        for c in cs:
            c.start()
        return cs

    over_layers(along_y(orb))
    beside[0].wait_recv()
    beside[1].wait_recv()
    over_layers(along_z(orb, zo))
    for c in entry[1:5]:
        c.wait_recv()

    def last_first(k):
        here = orb[k + 6]
        h = acc[k] + part_x(orb, k + 6)
        first[k + 6] = (h - filter_center * here) * (1.0 / filter_half)

    over_layers(last_first)

    rims = rims_of(first, 0)
    beside.append(to_mate(2, first.at[mid], zf))
    over_layers(along_y(first))
    beside[2].wait_recv()
    over_layers(along_z(first, zf))
    for c in rims:
        c.wait_recv()

    def last_filtered(k):
        here = first[k + 6]
        h = acc[k] + part_x(first, k + 6)
        fil[k + 6] = (h - filter_center * here) * (2.0 / filter_half) - orb[k + 6]

    over_layers(last_filtered)

    rims += rims_of(fil, 2)
    beside.append(to_mate(3, fil.at[mid], zs))

    def turn(j):
        pz = (z + far_first(j // 2, 4)) % 8
        return pz, (y // 4 + 1 + j) % 2

    def send_tiles(src, skip, got, which, pz, py_half, count):
        for i in range(count):
            py = py_half * 4 + (y + 1 + i) % 4
            rdma(
                src.at[skip + pz * 2 + py_half, pl.ds(pl.multiple_of((py % 4) * 8, 8), 8)], got.at[zy],
                a2a_send.at[which], a2a_recv.at[which], at(pz, py, x, core),
            ).start()

    def keep_tile(src, skip, got):
        got[zy] = src[skip + zy // 4, pl.ds(pl.multiple_of((zy % 4) * 8, 8), 8)]

    def all_tiles(got, which):
        return rdma(got.at[pl.ds(0, 63)], got.at[pl.ds(0, 63)], a2a_send.at[which], a2a_recv.at[which], mate)

    def filtered_out(j, _):
        pz, half = turn(j)
        send_tiles(fil, 6, gf, 0, pz, half, 4)
        acc[j] = part_y(fil[j + 6], pot[j])
        return 0

    lax.fori_loop(0, CX - 1, filtered_out, 0)
    send_tiles(fil, 6, gf, 0, z, y // 4, 3)
    keep_tile(fil, 6, gf)
    acc[CX - 1] = part_y(fil[CX + 5], pot[CX - 1])

    beside[3].wait_recv()
    over_layers(along_z(fil, zs))
    for c in rims[2:]:
        c.wait_recv()

    def applied_layer(k):
        hf[k] = acc[k] + part_x(fil, k + 6)

    def applied_out(j, _):
        pz, half = turn(j)
        applied_layer(pz * 2 + half)
        send_tiles(hf, 0, gh, 1, pz, half, 4)
        return 0

    lax.fori_loop(0, CX - 1, applied_out, 0)
    applied_layer(zy // 4)
    send_tiles(hf, 0, gh, 1, z, y // 4, 3)
    keep_tile(hf, 0, gh)

    def contract(left, right):
        return lax.dot_general(
            left, right, (((1,), (1,)), ((), ())),
            precision=lax.Precision.HIGHEST, preferred_element_type=jnp.float32,
        )

    all_tiles(gf, 0).wait_recv()
    all_tiles(gh, 1).wait_recv()

    back = rdma(fil.at[mid, rows_other], out_f.at[yl], back_send, back_recv, at(z, yo, x, core))
    back.start()
    keep = pltpu.make_async_copy(fil.at[mid, rows], out_f.at[yl], loc_sem.at[2])
    keep.start()

    both = jnp.zeros((NB, 2 * NB), jnp.float32)
    for s in range(8):
        left = gf[:, s, :]
        both = both + contract(left, jnp.concatenate([left, gh[:, s, :]], axis=0))
    part[...] = both.reshape(8, 8, 2 * NB)

    slot = z * 2 + yl

    def send_rows(j, _):
        pz, py = (z + far_first(j // 2, 4)) % 8, (yl + 1 + j) % 2
        rdma(
            part.at[pz], r1.at[slot], red_send.at[0], red_recv.at[0],
            (pz * 4 + yh, x * 4 + py * 2 + core),
        ).start()
        return 0

    lax.fori_loop(0, 15, send_rows, 0)
    r1[slot] = part[z]
    red1 = rdma(r1.at[pl.ds(0, 15)], r1.at[pl.ds(0, 15)], red_send.at[0], red_recv.at[0], mate)
    red1.wait_recv()

    total = jnp.sum(r1[...], axis=0)
    for i in range(4):
        tot[i] = total[2 * i : 2 * i + 2]
    slot2 = yh * 8 + x * 2 + core

    def send_total(j, _):
        ph, px = (yh + far_first(j // 8, 2)) % 4, (x + far_first((j // 2) % 4, 2)) % 4
        rdma(
            tot.at[ph], r2.at[slot2], red_send.at[1], red_recv.at[1],
            (z * 4 + ph, px * 4 + yl * 2 + (core + 1 + j) % 2),
        ).start()
        return 0

    lax.fori_loop(0, 31, send_total, 0)
    r2[slot2] = tot[yh]
    red2 = rdma(r2.at[pl.ds(0, 31)], r2.at[pl.ds(0, 31)], red_send.at[1], red_recv.at[1], mate)
    red2.wait_recv()
    result = jnp.sum(r2[...], axis=0) * (1.0 / NCELL)
    out_s[...] = result[:, :NB]
    out_p[...] = result[:, NB:]

    for c in entry:
        c.wait_send()
    for c in beside:
        c.wait_send()
    for c in rims:
        c.wait_send()
    all_tiles(gf, 0).wait_send()
    all_tiles(gh, 1).wait_send()
    red1.wait_send()
    red2.wait_send()
    keep.wait()
    back.wait()


def shards(orbitals, potential):
    f32 = jnp.float32
    vmem = pltpu.VMEM
    dma = pltpu.SemaphoreType.DMA
    hbm = pl.BlockSpec(memory_space=pltpu.HBM)
    full = pl.BlockSpec(memory_space=pltpu.VMEM)
    filtered, inter, proj = pl.pallas_call(
        kernel,
        out_shape=(
            jax.ShapeDtypeStruct((2, CX, CY, CZ), f32),
            jax.ShapeDtypeStruct((2, NB), f32),
            jax.ShapeDtypeStruct((2, NB), f32),
        ),
        in_specs=[hbm, hbm],
        out_specs=(hbm, full, full),
        scratch_shapes=[
            vmem((CX + 12, NY, CZ), f32),
            vmem((CX, NY, CZ), f32),
            vmem((CX + 12, NY, CZ), f32),
            vmem((CX + 12, NY, CZ), f32),
            vmem((CX, NY, CZ), f32),
            vmem((CX, NY, CZ), f32),
            vmem((CX, NY, CZ), f32),
            vmem((CX, NY, CZ), f32),
            vmem((CX, NY, CZ), f32),
            vmem((NB, 8, CZ), f32),
            vmem((NB, 8, CZ), f32),
            vmem((8, 8, 2 * NB), f32),
            vmem((16, 8, 2 * NB), f32),
            vmem((32, 2, 2 * NB), f32),
            vmem((4, 2, 2 * NB), f32),
            dma((3,)), dma((6,)), dma((6,)), dma((4,)), dma((4,)), dma((4,)), dma((4,)),
            dma((2,)), dma((2,)), dma, dma, dma((2,)), dma((2,)),
        ],
        compiler_params=pltpu.CompilerParams(
            collective_id=0, has_side_effects=True, vmem_limit_bytes=60 << 20
        ),
        name="chebyshev_step",
    )(orbitals.reshape(2, CX, CY, CZ), potential.reshape(CX, CY, CZ))
    return filtered[:, None], inter, proj


def solution(mesh):
    return jax.shard_map(
        shards,
        mesh=mesh,
        in_specs=(P("band", "domain", None, None, None), P("domain", None, None, None)),
        out_specs=(P("band", "domain", None, None, None), P("band", None), P("band", None)),
        check_vma=False,
    )
```

```python
import functools

import jax
import jax.numpy as jnp
from jax import lax
from jax.experimental import pallas as pl
from jax.experimental.pallas import tpu as pltpu
from jax.sharding import PartitionSpec as P

second_coeffs = (
    -5369.0 / 1800.0,
    12.0 / 7.0,
    -15.0 / 56.0,
    10.0 / 189.0,
    -1.0 / 112.0,
    2.0 / 1925.0,
    -1.0 / 16632.0,
)
filter_center = 6.5
filter_half = 5.5
reach = 6
MESH = pl.DeviceIdType.MESH

CX, CY, CZ = 16, 16, 128
NY = 32
NB = 64
NCELL = 524288


def part_y(here):
    total = (-1.5 * second_coeffs[0]) * here
    for s in range(1, reach + 1):
        pair = pltpu.roll(here, s, 0) + pltpu.roll(here, NY - s, 0)
        total = total + (-0.5 * second_coeffs[s]) * pair
    return total


def part_z(here, beside, lane):
    total = None
    for s in range(1, reach + 1):
        ahead = pltpu.roll(jnp.where(lane < s, beside, here), CZ - s, 1)
        behind = pltpu.roll(jnp.where(lane >= CZ - s, beside, here), s, 1)
        term = (-0.5 * second_coeffs[s]) * (ahead + behind)
        total = term if total is None else total + term
    return total


def part_x(src, j):
    total = None
    for s in range(1, reach + 1):
        term = (-0.5 * second_coeffs[s]) * (src[j + s] + src[j - s])
        total = term if total is None else total + term
    return total


def far_first(i, half):
    return half + ((i + 1) // 2) * (2 * (i % 2) - 1)


def kernel(
    orb_in, pot_in, out_f, out_sp,
    orb, pot, first, fil, zo, zf, zs, acc, hf, gf, gh, part, r1, r2, tot,
    loc_sem, in_send, in_recv, core_send, core_recv, x_send, x_recv,
    a2a_send, a2a_recv, back_send, back_recv, red_send, red_recv, ring,
):
    band = lax.axis_index("band")
    domain = lax.axis_index("domain")
    z, yh = band // 4, band % 4
    x, yl, core = domain // 4, (domain // 2) % 2, domain % 2
    y = yh * 2 + yl
    zy = z * 8 + y
    mine = pl.multiple_of(yl * CY, CY)
    other = pl.multiple_of((1 - yl) * CY, CY)

    def at(pz, py, px, pc):
        return (pz * 4 + py // 2, px * 4 + (py % 2) * 2 + pc)

    xn, xp = (x + 1) % 4, (x + 3) % 4
    yo = y + 1 - 2 * yl
    yq = (y + 7 + 2 * yl) % 8
    mate = at(z, y, x, 1 - core)
    to_xn, to_xp = at(z, y, xn, core), at(z, y, xp, core)

    def rdma(src, dst, send, recv, to):
        return pltpu.make_async_remote_copy(
            src_ref=src, dst_ref=dst, send_sem=send, recv_sem=recv,
            device_id=to, device_id_type=MESH,
        )

    mid = pl.ds(6, CX)
    low, high = pl.ds(0, 6), pl.ds(22, 6)
    rows = pl.ds(mine, CY)
    rows_other = pl.ds(other, CY)

    local = [
        pltpu.make_async_copy(orb_in.at[yl], orb.at[mid, rows], loc_sem.at[0]),
        pltpu.make_async_copy(pot_in, pot.at[:, rows], loc_sem.at[1]),
    ]
    for c in local:
        c.start()

    bar = pltpu.get_barrier_semaphore()
    up_z, down_z = at((z + 1) % 8, y, x, core), at((z + 7) % 8, y, x, core)
    up_y, down_y = at(z, (y + 1) % 8, x, core), at(z, (y + 7) % 8, x, core)
    for to in (up_y, down_y, to_xn, to_xp, up_z, down_z, mate):
        pl.semaphore_signal(bar, inc=1, device_id=to, device_id_type=MESH)
    pl.semaphore_wait(bar, 7)

    far_z = (at((z + 2) % 8, y, x, core), at((z + 6) % 8, y, x, core))
    far_y = (at(z, (y + 2) % 8, x, core), at(z, (y + 6) % 8, x, core))
    words = (
        (up_z, down_z), far_z, (up_y, down_y), (up_y, down_y), far_y, (mate,), (to_xn, to_xp), (to_xn, to_xp),
    )

    def tell(k):
        for to in words[k]:
            pl.semaphore_signal(ring.at[k], inc=1, device_id=to, device_id_type=MESH)

    def hear(k):
        pl.semaphore_wait(ring.at[k], len(words[k]))

    swaps = [
        rdma(
            orb_in.at[1 - yl, pl.ds(k, n)], orb.at[pl.ds(k + 6, n), rows],
            in_send.at[i], in_recv.at[i], at(z, yo, x, core),
        )
        for i, (k, n) in enumerate(((0, 6), (10, 6), (6, 4)))
    ]
    direct = [
        rdma(orb_in.at[yl, pl.ds(10, 6)], orb.at[low, rows], in_send.at[3], in_recv.at[3], to_xn),
        rdma(orb_in.at[yl, pl.ds(0, 6)], orb.at[high, rows], in_send.at[4], in_recv.at[4], to_xp),
    ]
    given = rdma(pot_in, pot.at[:, rows], in_send.at[5], in_recv.at[5], at(z, yq, x, core))

    def to_mate(k, src, dst):
        c = rdma(src, dst, core_send.at[k], core_recv.at[k], mate)
        c.start()
        return c

    beside = [to_mate(0, orb_in.at[yl], zo.at[:, rows])]
    for c in swaps + direct + [given]:
        c.start()
    tell(0)
    for c in local:
        c.wait()

    lane = lax.broadcasted_iota(jnp.int32, (NY, CZ), 1)
    lane_half = lax.broadcasted_iota(jnp.int32, (CY, CZ), 1)

    def over_layers(body, first_layer=0, count=CX):
        def step(k, _):
            body(k)
            return 0

        lax.fori_loop(first_layer, first_layer + count, step, 0)

    def along_y(src):
        def body(k):
            acc[k] = part_y(src[k + 6])

        return body

    def along_z(src, beside_src):
        def body(k):
            acc[k] = acc[k] + part_z(src[k + 6], beside_src[k], lane)

        return body

    def along_z_half(at_rows):
        def body(k):
            hf[k, at_rows] = part_z(orb[k + 6, at_rows], zo[k, at_rows], lane_half)

        return body

    def rim(src, k, to_next, at_rows=slice(None)):
        if to_next:
            c = rdma(src.at[pl.ds(16, 6), at_rows], src.at[low, at_rows], x_send.at[k], x_recv.at[k], to_xn)
        else:
            c = rdma(src.at[pl.ds(6, 6), at_rows], src.at[high, at_rows], x_send.at[k], x_recv.at[k], to_xp)
        c.start()
        return c

    beside[0].wait_recv()
    over_layers(along_z_half(rows))
    hear(0)
    tell(1)
    swaps[0].wait_recv()
    rims = [rim(orb, 0, False, rows_other)]
    swaps[1].wait_recv()
    rims.append(rim(orb, 1, True, rows_other))
    swaps[2].wait_recv()
    beside.append(to_mate(1, orb.at[mid, rows_other], zo.at[:, rows_other]))
    over_layers(along_y(orb))
    hear(1)
    tell(2)
    beside[1].wait_recv()
    over_layers(along_z_half(rows_other))
    given.wait_recv()
    for c in direct + rims:
        c.wait_recv()

    def by_edges(body, src, k):
        over_layers(body, 0, 6)
        sent = [rim(src, k, False)]
        over_layers(body, 10, 6)
        sent.append(rim(src, k + 1, True))
        over_layers(body, 6, 4)
        beside.append(to_mate(k // 2 + 1, src.at[mid], zf if k == 2 else zs))
        return sent

    def last_first(k):
        here = orb[k + 6]
        h = acc[k] + hf[k] + part_x(orb, k + 6) + (pot[k] - filter_center) * here
        first[k + 6] = h * (1.0 / filter_half)

    rims += by_edges(last_first, first, 2)

    hear(2)
    tell(3)
    over_layers(along_y(first))
    hear(3)
    tell(4)
    beside[2].wait_recv()
    over_layers(along_z(first, zf))
    hear(4)
    tell(5)
    for c in rims[2:]:
        c.wait_recv()

    def last_filtered(k):
        here = first[k + 6]
        h = acc[k] + part_x(first, k + 6) + (pot[k] - filter_center) * here
        fil[k + 6] = h * (2.0 / filter_half) - orb[k + 6]

    rims += by_edges(last_filtered, fil, 4)

    def turn(j):
        pz = (z + far_first(j // 2, 4)) % 8
        return pz, (y // 4 + 1 + j) % 2

    def send_tiles(src, skip, got, which, pz, py_half, count):
        for i in range(count):
            py = py_half * 4 + (y + 1 + i) % 4
            rdma(
                src.at[skip + pz * 2 + py_half, pl.ds(pl.multiple_of((py % 4) * 8, 8), 8)], got.at[zy],
                a2a_send.at[which], a2a_recv.at[which], at(pz, py, x, core),
            ).start()

    def keep_tile(src, skip, got):
        got[zy] = src[skip + zy // 4, pl.ds(pl.multiple_of((zy % 4) * 8, 8), 8)]

    def all_tiles(got, which):
        return rdma(got.at[pl.ds(0, 63)], got.at[pl.ds(0, 63)], a2a_send.at[which], a2a_recv.at[which], mate)

    def filtered_out(j, _):
        pz, half = turn(j)
        send_tiles(fil, 6, gf, 0, pz, half, 4)
        acc[j] = part_y(fil[j + 6])
        return 0

    lax.fori_loop(0, CX - 1, filtered_out, 0)
    send_tiles(fil, 6, gf, 0, z, y // 4, 3)
    keep_tile(fil, 6, gf)
    acc[CX - 1] = part_y(fil[CX + 5])
    hear(5)
    tell(6)

    beside[3].wait_recv()
    over_layers(along_z(fil, zs))
    hear(6)
    tell(7)
    for c in rims[4:]:
        c.wait_recv()

    def applied_layer(k):
        hf[k] = acc[k] + part_x(fil, k + 6) + pot[k] * fil[k + 6]

    def applied_out(j, _):
        pz, half = turn(j)
        applied_layer(pz * 2 + half)
        send_tiles(hf, 0, gh, 1, pz, half, 4)
        return 0

    lax.fori_loop(0, CX - 1, applied_out, 0)
    applied_layer(zy // 4)
    send_tiles(hf, 0, gh, 1, z, y // 4, 3)
    keep_tile(hf, 0, gh)

    def contract(left, right):
        return lax.dot_general(
            left, right, (((1,), (1,)), ((), ())),
            precision=lax.Precision.HIGHEST, preferred_element_type=jnp.float32,
        )

    hear(7)
    all_tiles(gf, 0).wait_recv()
    over = jnp.zeros((NB, NB), jnp.float32)
    for s in range(8):
        over = over + contract(gf[:, s, :], gf[:, s, :])
    part[:, :, :NB] = over.reshape(8, 8, NB)
    all_tiles(gh, 1).wait_recv()
    proj = jnp.zeros((NB, NB), jnp.float32)
    for s in range(8):
        proj = proj + contract(gf[:, s, :], gh[:, s, :])
    part[:, :, NB:] = proj.reshape(8, 8, NB)

    slot = z * 2 + yl

    def send_rows(j, _):
        pz, py = (z + far_first(j // 2, 4)) % 8, (yl + 1 + j) % 2
        rdma(
            part.at[pz], r1.at[slot], red_send.at[0], red_recv.at[0],
            (pz * 4 + yh, x * 4 + py * 2 + core),
        ).start()
        return 0

    lax.fori_loop(0, 15, send_rows, 0)
    back = rdma(fil.at[mid, rows_other], out_f.at[yl], back_send, back_recv, at(z, yo, x, core))
    back.start()
    keep = pltpu.make_async_copy(fil.at[mid, rows], out_f.at[yl], loc_sem.at[2])
    keep.start()
    r1[slot] = part[z]
    red1 = rdma(r1.at[pl.ds(0, 15)], r1.at[pl.ds(0, 15)], red_send.at[0], red_recv.at[0], mate)
    red1.wait_recv()

    total = jnp.sum(r1[...], axis=0)
    for i in range(4):
        tot[i] = total[2 * i : 2 * i + 2]
    slot2 = yh * 8 + x * 2 + core

    def send_total(j, _):
        ph, px = (yh + far_first(j // 8, 2)) % 4, (x + far_first((j // 2) % 4, 2)) % 4
        rdma(
            tot.at[ph], r2.at[slot2], red_send.at[1], red_recv.at[1],
            (z * 4 + ph, px * 4 + yl * 2 + (core + 1 + j) % 2),
        ).start()
        return 0

    lax.fori_loop(0, 31, send_total, 0)
    r2[slot2] = tot[yh]
    red2 = rdma(r2.at[pl.ds(0, 31)], r2.at[pl.ds(0, 31)], red_send.at[1], red_recv.at[1], mate)
    red2.wait_recv()
    out_sp[...] = jnp.sum(r2[...], axis=0) * (1.0 / NCELL)

    for c in swaps + direct + [given]:
        c.wait_send()
    for c in beside:
        c.wait_send()
    for c in rims:
        c.wait_send()
    all_tiles(gf, 0).wait_send()
    all_tiles(gh, 1).wait_send()
    red1.wait_send()
    red2.wait_send()
    keep.wait()
    back.wait()


def deliver(filtered, both, out_f, out_s, out_p, sem):
    whole = pltpu.make_async_copy(filtered, out_f, sem)
    whole.start()
    out_s[...] = both[:, :NB]
    out_p[...] = both[:, NB:]
    whole.wait()


def shards(orbitals, potential):
    f32 = jnp.float32
    vmem = pltpu.VMEM
    dma = pltpu.SemaphoreType.DMA
    hbm = pl.BlockSpec(memory_space=pltpu.HBM)
    full = pl.BlockSpec(memory_space=pltpu.VMEM)
    filtered, both = pl.pallas_call(
        kernel,
        out_shape=(
            jax.ShapeDtypeStruct((2, CX, CY, CZ), f32),
            jax.ShapeDtypeStruct((2, 2 * NB), f32),
        ),
        in_specs=[hbm, hbm],
        out_specs=(hbm, full),
        scratch_shapes=[
            vmem((CX + 12, NY, CZ), f32),
            vmem((CX, NY, CZ), f32),
            vmem((CX + 12, NY, CZ), f32),
            vmem((CX + 12, NY, CZ), f32),
            vmem((CX, NY, CZ), f32),
            vmem((CX, NY, CZ), f32),
            vmem((CX, NY, CZ), f32),
            vmem((CX, NY, CZ), f32),
            vmem((CX, NY, CZ), f32),
            vmem((NB, 8, CZ), f32),
            vmem((NB, 8, CZ), f32),
            vmem((8, 8, 2 * NB), f32),
            vmem((16, 8, 2 * NB), f32),
            vmem((32, 2, 2 * NB), f32),
            vmem((4, 2, 2 * NB), f32),
            dma((3,)), dma((6,)), dma((6,)), dma((4,)), dma((4,)), dma((6,)), dma((6,)),
            dma((2,)), dma((2,)), dma, dma, dma((2,)), dma((2,)),
            pltpu.SemaphoreType.REGULAR((8,)),
        ],
        compiler_params=pltpu.CompilerParams(
            collective_id=0, has_side_effects=True, vmem_limit_bytes=60 << 20
        ),
        name="chebyshev_step",
    )(orbitals.reshape(2, CX, CY, CZ), potential.reshape(CX, CY, CZ))
    filtered, inter, proj = pl.pallas_call(
        deliver,
        out_shape=(
            jax.ShapeDtypeStruct((2, CX, CY, CZ), f32),
            jax.ShapeDtypeStruct((2, NB), f32),
            jax.ShapeDtypeStruct((2, NB), f32),
        ),
        in_specs=[hbm, full],
        out_specs=(hbm, full, full),
        scratch_shapes=[dma],
        compiler_params=pltpu.CompilerParams(vmem_limit_bytes=60 << 20),
        name="deliver",
    )(filtered, both)
    return filtered[:, None], inter, proj


def solution(mesh):
    return jax.shard_map(
        shards,
        mesh=mesh,
        in_specs=(P("band", "domain", None, None, None), P("domain", None, None, None)),
        out_specs=(P("band", "domain", None, None, None), P("band", None), P("band", None)),
        check_vma=False,
    )
```

```python
import functools

import jax
import jax.numpy as jnp
from jax import lax
from jax.experimental import pallas as pl
from jax.experimental.pallas import tpu as pltpu
from jax.sharding import PartitionSpec as P

second_coeffs = (
    -5369.0 / 1800.0,
    12.0 / 7.0,
    -15.0 / 56.0,
    10.0 / 189.0,
    -1.0 / 112.0,
    2.0 / 1925.0,
    -1.0 / 16632.0,
)
filter_center = 6.5
filter_half = 5.5
reach = 6
MESH = pl.DeviceIdType.MESH

CX, CY, CZ = 16, 16, 128
NY = 32
NB = 64
NCELL = 524288


def part_y(here):
    total = (-1.5 * second_coeffs[0]) * here
    for s in range(1, reach + 1):
        pair = pltpu.roll(here, s, 0) + pltpu.roll(here, NY - s, 0)
        total = total + (-0.5 * second_coeffs[s]) * pair
    return total


def part_z(here, beside, lane):
    total = None
    for s in range(1, reach + 1):
        ahead = pltpu.roll(jnp.where(lane < s, beside, here), CZ - s, 1)
        behind = pltpu.roll(jnp.where(lane >= CZ - s, beside, here), s, 1)
        term = (-0.5 * second_coeffs[s]) * (ahead + behind)
        total = term if total is None else total + term
    return total


def part_x(src, j):
    total = None
    for s in range(1, reach + 1):
        term = (-0.5 * second_coeffs[s]) * (src[j + s] + src[j - s])
        total = term if total is None else total + term
    return total


def far_first(i, half):
    return half + ((i + 1) // 2) * (2 * (i % 2) - 1)


def kernel(
    orb_in, pot_in, out_f, out_sp,
    orb, pot, first, fil, zo, zf, zs, acc, hf, gf, gh, part, r1, r2, tot,
    loc_sem, in_send, in_recv, core_send, core_recv, x_send, x_recv,
    a2a_send, a2a_recv, back_send, back_recv, red_send, red_recv, ring,
):
    band = lax.axis_index("band")
    domain = lax.axis_index("domain")
    z, yh = band // 4, band % 4
    x, yl, core = domain // 4, (domain // 2) % 2, domain % 2
    y = yh * 2 + yl
    zy = z * 8 + y
    mine = pl.multiple_of(yl * CY, CY)
    other = pl.multiple_of((1 - yl) * CY, CY)

    def at(pz, py, px, pc):
        return (pz * 4 + py // 2, px * 4 + (py % 2) * 2 + pc)

    xn, xp = (x + 1) % 4, (x + 3) % 4
    yo = y + 1 - 2 * yl
    yq = (y + 7 + 2 * yl) % 8
    mate = at(z, y, x, 1 - core)
    to_xn, to_xp = at(z, y, xn, core), at(z, y, xp, core)

    def rdma(src, dst, send, recv, to):
        return pltpu.make_async_remote_copy(
            src_ref=src, dst_ref=dst, send_sem=send, recv_sem=recv,
            device_id=to, device_id_type=MESH,
        )

    mid = pl.ds(6, CX)
    low, high = pl.ds(0, 6), pl.ds(22, 6)
    rows = pl.ds(mine, CY)
    rows_other = pl.ds(other, CY)

    local = [
        pltpu.make_async_copy(orb_in.at[yl], orb.at[mid, rows], loc_sem.at[0]),
        pltpu.make_async_copy(pot_in, pot.at[:, rows], loc_sem.at[1]),
    ]
    for c in local:
        c.start()

    bar = pltpu.get_barrier_semaphore()
    up_z, down_z = at((z + 1) % 8, y, x, core), at((z + 7) % 8, y, x, core)
    up_y, down_y = at(z, (y + 1) % 8, x, core), at(z, (y + 7) % 8, x, core)
    for to in (up_y, down_y, to_xn, to_xp, up_z, down_z, mate):
        pl.semaphore_signal(bar, inc=1, device_id=to, device_id_type=MESH)
    pl.semaphore_wait(bar, 7)

    far_z = (at((z + 2) % 8, y, x, core), at((z + 6) % 8, y, x, core))
    far_y = (at(z, (y + 2) % 8, x, core), at(z, (y + 6) % 8, x, core))
    words = (
        (up_z, down_z), far_z, (up_y, down_y), (up_y, down_y), far_y, (mate,), (to_xn, to_xp), (to_xn, to_xp),
    )

    def tell(k):
        for to in words[k]:
            pl.semaphore_signal(ring.at[k], inc=1, device_id=to, device_id_type=MESH)

    def hear(k):
        pl.semaphore_wait(ring.at[k], len(words[k]))

    swaps = [
        rdma(
            orb_in.at[1 - yl, pl.ds(k, n)], orb.at[pl.ds(k + 6, n), rows],
            in_send.at[i], in_recv.at[i], at(z, yo, x, core),
        )
        for i, (k, n) in enumerate(((0, 6), (10, 6), (6, 4)))
    ]
    direct = [
        rdma(orb_in.at[yl, pl.ds(10, 6)], orb.at[low, rows], in_send.at[3], in_recv.at[3], to_xn),
        rdma(orb_in.at[yl, pl.ds(0, 6)], orb.at[high, rows], in_send.at[4], in_recv.at[4], to_xp),
    ]
    given = rdma(pot_in, pot.at[:, rows], in_send.at[5], in_recv.at[5], at(z, yq, x, core))

    def to_mate(k, src, dst):
        c = rdma(src, dst, core_send.at[k], core_recv.at[k], mate)
        c.start()
        return c

    beside = [to_mate(0, orb_in.at[yl], zo.at[:, rows])]
    for c in swaps + direct + [given]:
        c.start()
    tell(0)
    for c in local:
        c.wait()

    lane = lax.broadcasted_iota(jnp.int32, (NY, CZ), 1)
    lane_half = lax.broadcasted_iota(jnp.int32, (CY, CZ), 1)

    def over_layers(body, first_layer=0, count=CX):
        def step(k, _):
            body(k)
            return 0

        lax.fori_loop(first_layer, first_layer + count, step, 0)

    def along_y(src):
        def body(k):
            acc[k] = part_y(src[k + 6])

        return body

    def along_z(src, beside_src):
        def body(k):
            acc[k] = acc[k] + part_z(src[k + 6], beside_src[k], lane)

        return body

    def along_z_half(at_rows):
        def body(k):
            hf[k, at_rows] = part_z(orb[k + 6, at_rows], zo[k, at_rows], lane_half)

        return body

    def rim(src, k, to_next, at_rows=slice(None)):
        if to_next:
            c = rdma(src.at[pl.ds(16, 6), at_rows], src.at[low, at_rows], x_send.at[k], x_recv.at[k], to_xn)
        else:
            c = rdma(src.at[pl.ds(6, 6), at_rows], src.at[high, at_rows], x_send.at[k], x_recv.at[k], to_xp)
        c.start()
        return c

    beside[0].wait_recv()
    over_layers(along_z_half(rows))
    hear(0)
    tell(1)
    swaps[0].wait_recv()
    rims = [rim(orb, 0, False, rows_other)]
    swaps[1].wait_recv()
    rims.append(rim(orb, 1, True, rows_other))
    swaps[2].wait_recv()
    beside.append(to_mate(1, orb.at[mid, rows_other], zo.at[:, rows_other]))
    over_layers(along_y(orb))
    hear(1)
    tell(2)
    beside[1].wait_recv()
    over_layers(along_z_half(rows_other))
    given.wait_recv()
    for c in direct + rims:
        c.wait_recv()

    def by_edges(body, src, k):
        over_layers(body, 0, 6)
        sent = [rim(src, k, False)]
        over_layers(body, 10, 6)
        sent.append(rim(src, k + 1, True))
        over_layers(body, 6, 4)
        beside.append(to_mate(k // 2 + 1, src.at[mid], zf if k == 2 else zs))
        return sent

    def last_first(k):
        here = orb[k + 6]
        h = acc[k] + hf[k] + part_x(orb, k + 6) + (pot[k] - filter_center) * here
        first[k + 6] = h * (1.0 / filter_half)

    rims += by_edges(last_first, first, 2)

    hear(2)
    tell(3)
    over_layers(along_y(first))
    hear(3)
    tell(4)
    beside[2].wait_recv()
    over_layers(along_z(first, zf))
    hear(4)
    tell(5)
    for c in rims[2:]:
        c.wait_recv()

    def last_filtered(k):
        here = first[k + 6]
        h = acc[k] + part_x(first, k + 6) + (pot[k] - filter_center) * here
        fil[k + 6] = h * (2.0 / filter_half) - orb[k + 6]

    rims += by_edges(last_filtered, fil, 4)

    def turn(j):
        pz = (z + far_first(j // 2, 4)) % 8
        return pz, (y // 4 + 1 + j) % 2

    def send_tiles(src, skip, got, which, pz, py_half, count):
        for i in range(count):
            py = py_half * 4 + (y + 1 + i) % 4
            rdma(
                src.at[skip + pz * 2 + py_half, pl.ds(pl.multiple_of((py % 4) * 8, 8), 8)], got.at[zy],
                a2a_send.at[which], a2a_recv.at[which], at(pz, py, x, core),
            ).start()

    def keep_tile(src, skip, got):
        got[zy] = src[skip + zy // 4, pl.ds(pl.multiple_of((zy % 4) * 8, 8), 8)]

    def all_tiles(got, which):
        return rdma(got.at[pl.ds(0, 63)], got.at[pl.ds(0, 63)], a2a_send.at[which], a2a_recv.at[which], mate)

    def filtered_out(j, _):
        pz, half = turn(j)
        send_tiles(fil, 6, gf, 0, pz, half, 4)
        acc[j] = part_y(fil[j + 6])
        return 0

    lax.fori_loop(0, CX - 1, filtered_out, 0)
    send_tiles(fil, 6, gf, 0, z, y // 4, 3)
    keep_tile(fil, 6, gf)
    acc[CX - 1] = part_y(fil[CX + 5])
    hear(5)
    tell(6)

    beside[3].wait_recv()
    over_layers(along_z(fil, zs))
    hear(6)
    tell(7)
    for c in rims[4:]:
        c.wait_recv()

    def applied_layer(k):
        hf[k] = acc[k] + part_x(fil, k + 6) + pot[k] * fil[k + 6]

    def applied_out(j, _):
        pz, half = turn(j)
        applied_layer(pz * 2 + half)
        send_tiles(hf, 0, gh, 1, pz, half, 4)
        return 0

    lax.fori_loop(0, CX - 1, applied_out, 0)
    applied_layer(zy // 4)
    send_tiles(hf, 0, gh, 1, z, y // 4, 3)
    keep_tile(hf, 0, gh)

    def contract(left, right):
        return lax.dot_general(
            left, right, (((1,), (1,)), ((), ())),
            precision=lax.Precision.HIGHEST, preferred_element_type=jnp.float32,
        )

    hear(7)
    all_tiles(gf, 0).wait_recv()
    over = jnp.zeros((NB, NB), jnp.float32)
    for s in range(8):
        over = over + contract(gf[:, s, :], gf[:, s, :])
    part[:, :, :NB] = over.reshape(8, 8, NB)
    all_tiles(gh, 1).wait_recv()
    proj = jnp.zeros((NB, NB), jnp.float32)
    for s in range(8):
        proj = proj + contract(gf[:, s, :], gh[:, s, :])
    part[:, :, NB:] = proj.reshape(8, 8, NB)

    slot = z * 2 + yl

    def send_rows(j, _):
        pz, py = (z + far_first(j // 2, 4)) % 8, (yl + 1 + j) % 2
        rdma(
            part.at[pz], r1.at[slot], red_send.at[0], red_recv.at[0],
            (pz * 4 + yh, x * 4 + py * 2 + core),
        ).start()
        return 0

    lax.fori_loop(0, 15, send_rows, 0)
    back = rdma(fil.at[mid, rows_other], out_f.at[yl], back_send, back_recv, at(z, yo, x, core))
    back.start()
    keep = pltpu.make_async_copy(fil.at[mid, rows], out_f.at[yl], loc_sem.at[2])
    keep.start()
    r1[slot] = part[z]
    red1 = rdma(r1.at[pl.ds(0, 15)], r1.at[pl.ds(0, 15)], red_send.at[0], red_recv.at[0], mate)
    red1.wait_recv()

    total = jnp.sum(r1[...], axis=0)
    for i in range(4):
        tot[i] = total[2 * i : 2 * i + 2]
    slot2 = yh * 8 + x * 2 + core

    def send_total(j, _):
        ph, px = (yh + far_first(j // 8, 2)) % 4, (x + far_first((j // 2) % 4, 2)) % 4
        rdma(
            tot.at[ph], r2.at[slot2], red_send.at[1], red_recv.at[1],
            (z * 4 + ph, px * 4 + yl * 2 + (core + 1 + j) % 2),
        ).start()
        return 0

    lax.fori_loop(0, 31, send_total, 0)
    r2[slot2] = tot[yh]
    red2 = rdma(r2.at[pl.ds(0, 31)], r2.at[pl.ds(0, 31)], red_send.at[1], red_recv.at[1], mate)
    red2.wait_recv()
    out_sp[...] = jnp.sum(r2[...], axis=0) * (1.0 / NCELL)

    for c in swaps + direct + [given]:
        c.wait_send()
    for c in beside:
        c.wait_send()
    for c in rims:
        c.wait_send()
    all_tiles(gf, 0).wait_send()
    all_tiles(gh, 1).wait_send()
    red1.wait_send()
    red2.wait_send()
    keep.wait()
    back.wait()


def deliver(filtered, both, out_f, out_s, out_p, sem):
    whole = pltpu.make_async_copy(filtered, out_f, sem)
    whole.start()
    out_s[...] = both[:, :NB]
    out_p[...] = both[:, NB:]
    whole.wait()


def shards(orbitals, potential):
    f32 = jnp.float32
    vmem = pltpu.VMEM
    dma = pltpu.SemaphoreType.DMA
    hbm = pl.BlockSpec(memory_space=pltpu.HBM)
    full = pl.BlockSpec(memory_space=pltpu.VMEM)
    filtered, both = pl.pallas_call(
        kernel,
        out_shape=(
            jax.ShapeDtypeStruct((2, CX, CY, CZ), f32),
            jax.ShapeDtypeStruct((2, 2 * NB), f32),
        ),
        in_specs=[hbm, hbm],
        out_specs=(hbm, full),
        scratch_shapes=[
            vmem((CX + 12, NY, CZ), f32),
            vmem((CX, NY, CZ), f32),
            vmem((CX + 12, NY, CZ), f32),
            vmem((CX + 12, NY, CZ), f32),
            vmem((CX, NY, CZ), f32),
            vmem((CX, NY, CZ), f32),
            vmem((CX, NY, CZ), f32),
            vmem((CX, NY, CZ), f32),
            vmem((CX, NY, CZ), f32),
            vmem((NB, 8, CZ), f32),
            vmem((NB, 8, CZ), f32),
            vmem((8, 8, 2 * NB), f32),
            vmem((16, 8, 2 * NB), f32),
            vmem((32, 2, 2 * NB), f32),
            vmem((4, 2, 2 * NB), f32),
            dma((3,)), dma((6,)), dma((6,)), dma((4,)), dma((4,)), dma((6,)), dma((6,)),
            dma((2,)), dma((2,)), dma, dma, dma((2,)), dma((2,)),
            pltpu.SemaphoreType.REGULAR((8,)),
        ],
        compiler_params=pltpu.CompilerParams(
            collective_id=0, has_side_effects=True, vmem_limit_bytes=32 << 20
        ),
        name="chebyshev_step",
    )(
        pltpu.with_memory_space_constraint(orbitals.reshape(2, CX, CY, CZ), pltpu.HBM),
        pltpu.with_memory_space_constraint(potential.reshape(CX, CY, CZ), pltpu.HBM),
    )
    filtered, inter, proj = pl.pallas_call(
        deliver,
        out_shape=(
            jax.ShapeDtypeStruct((2, CX, CY, CZ), f32),
            jax.ShapeDtypeStruct((2, NB), f32),
            jax.ShapeDtypeStruct((2, NB), f32),
        ),
        in_specs=[pl.BlockSpec(memory_space=pl.ANY), full],
        out_specs=(hbm, full, full),
        scratch_shapes=[dma],
        compiler_params=pltpu.CompilerParams(vmem_limit_bytes=32 << 20),
        name="deliver",
    )(filtered, both)
    return filtered[:, None], inter, proj


def solution(mesh):
    return jax.shard_map(
        shards,
        mesh=mesh,
        in_specs=(P("band", "domain", None, None, None), P("domain", None, None, None)),
        out_specs=(P("band", "domain", None, None, None), P("band", None), P("band", None)),
        check_vma=False,
    )
```

```python
import functools

import jax
import jax.numpy as jnp
from jax import lax
from jax.experimental import pallas as pl
from jax.experimental.pallas import tpu as pltpu
from jax.sharding import PartitionSpec as P

second_coeffs = (
    -5369.0 / 1800.0,
    12.0 / 7.0,
    -15.0 / 56.0,
    10.0 / 189.0,
    -1.0 / 112.0,
    2.0 / 1925.0,
    -1.0 / 16632.0,
)
filter_center = 6.5
filter_half = 5.5
reach = 6
MESH = pl.DeviceIdType.MESH

CX, CY, CZ = 16, 16, 128
NY = 32
NB = 64
NCELL = 524288


def part_y(here):
    total = (-1.5 * second_coeffs[0]) * here
    for s in range(1, reach + 1):
        pair = pltpu.roll(here, s, 0) + pltpu.roll(here, NY - s, 0)
        total = total + (-0.5 * second_coeffs[s]) * pair
    return total


def part_z(here, beside, lane):
    total = None
    for s in range(1, reach + 1):
        ahead = pltpu.roll(jnp.where(lane < s, beside, here), CZ - s, 1)
        behind = pltpu.roll(jnp.where(lane >= CZ - s, beside, here), s, 1)
        term = (-0.5 * second_coeffs[s]) * (ahead + behind)
        total = term if total is None else total + term
    return total


def part_x(src, j):
    total = None
    for s in range(1, reach + 1):
        term = (-0.5 * second_coeffs[s]) * (src[j + s] + src[j - s])
        total = term if total is None else total + term
    return total


def far_first(i, half):
    return half + ((i + 1) // 2) * (2 * (i % 2) - 1)


def kernel(
    orb_in, pot_in, out_f, out_s, out_p,
    orb, pot, first, fil, zo, zf, zs, acc, hf, gf, gh, g_high, g_low, part, r1, r2, tot,
    loc_sem, in_send, in_recv, core_send, core_recv, x_send, x_recv,
    a2a_send, a2a_recv, back_send, back_recv, red_send, red_recv, ring,
):
    band = lax.axis_index("band")
    domain = lax.axis_index("domain")
    z, yh = band // 4, band % 4
    x, yl, core = domain // 4, (domain // 2) % 2, domain % 2
    y = yh * 2 + yl
    zy = z * 8 + y
    mine = pl.multiple_of(yl * CY, CY)
    other = pl.multiple_of((1 - yl) * CY, CY)

    def at(pz, py, px, pc):
        return (pz * 4 + py // 2, px * 4 + (py % 2) * 2 + pc)

    xn, xp = (x + 1) % 4, (x + 3) % 4
    yo = y + 1 - 2 * yl
    yq = (y + 7 + 2 * yl) % 8
    mate = at(z, y, x, 1 - core)
    to_xn, to_xp = at(z, y, xn, core), at(z, y, xp, core)

    def rdma(src, dst, send, recv, to):
        return pltpu.make_async_remote_copy(
            src_ref=src, dst_ref=dst, send_sem=send, recv_sem=recv,
            device_id=to, device_id_type=MESH,
        )

    mid = pl.ds(6, CX)
    low, high = pl.ds(0, 6), pl.ds(22, 6)
    rows = pl.ds(mine, CY)
    rows_other = pl.ds(other, CY)

    local = [
        pltpu.make_async_copy(orb_in.at[yl], orb.at[mid, rows], loc_sem.at[0]),
        pltpu.make_async_copy(pot_in, pot.at[:, rows], loc_sem.at[1]),
    ]
    for c in local:
        c.start()

    bar = pltpu.get_barrier_semaphore()
    up_z, down_z = at((z + 1) % 8, y, x, core), at((z + 7) % 8, y, x, core)
    up_y, down_y = at(z, (y + 1) % 8, x, core), at(z, (y + 7) % 8, x, core)
    for to in (up_y, down_y, to_xn, to_xp, up_z, down_z, mate):
        pl.semaphore_signal(bar, inc=1, device_id=to, device_id_type=MESH)
    pl.semaphore_wait(bar, 7)

    far_z = (at((z + 2) % 8, y, x, core), at((z + 6) % 8, y, x, core))
    far_y = (at(z, (y + 2) % 8, x, core), at(z, (y + 6) % 8, x, core))
    words = (
        (up_z, down_z), far_z, (up_y, down_y), (up_y, down_y), far_y, (mate,), (to_xn, to_xp), (to_xn, to_xp),
    )

    def tell(k):
        for to in words[k]:
            pl.semaphore_signal(ring.at[k], inc=1, device_id=to, device_id_type=MESH)

    def hear(k):
        pl.semaphore_wait(ring.at[k], len(words[k]))

    swaps = [
        rdma(
            orb_in.at[1 - yl, pl.ds(k, n)], orb.at[pl.ds(k + 6, n), rows],
            in_send.at[i], in_recv.at[i], at(z, yo, x, core),
        )
        for i, (k, n) in enumerate(((0, 6), (10, 6), (6, 4)))
    ]
    direct = [
        rdma(orb_in.at[yl, pl.ds(10, 6)], orb.at[low, rows], in_send.at[3], in_recv.at[3], to_xn),
        rdma(orb_in.at[yl, pl.ds(0, 6)], orb.at[high, rows], in_send.at[4], in_recv.at[4], to_xp),
    ]
    given = rdma(pot_in, pot.at[:, rows], in_send.at[5], in_recv.at[5], at(z, yq, x, core))

    def to_mate(k, src, dst):
        c = rdma(src, dst, core_send.at[k], core_recv.at[k], mate)
        c.start()
        return c

    beside = [to_mate(0, orb_in.at[yl], zo.at[:, rows])]
    for c in swaps[:2] + direct + [given]:
        c.start()
    tell(0)
    for c in local:
        c.wait()

    lane = lax.broadcasted_iota(jnp.int32, (NY, CZ), 1)
    lane_half = lax.broadcasted_iota(jnp.int32, (CY, CZ), 1)

    def over_layers(body, first_layer=0, count=CX):
        def step(k, _):
            body(k)
            return 0

        lax.fori_loop(first_layer, first_layer + count, step, 0)

    def along_y(src):
        def body(k):
            acc[k] = part_y(src[k + 6])

        return body

    def along_z(src, beside_src):
        def body(k):
            acc[k] = acc[k] + part_z(src[k + 6], beside_src[k], lane)

        return body

    def along_z_half(at_rows):
        def body(k):
            hf[k, at_rows] = part_z(orb[k + 6, at_rows], zo[k, at_rows], lane_half)

        return body

    def rim(src, k, to_next, at_rows=slice(None)):
        if to_next:
            c = rdma(src.at[pl.ds(16, 6), at_rows], src.at[low, at_rows], x_send.at[k], x_recv.at[k], to_xn)
        else:
            c = rdma(src.at[pl.ds(6, 6), at_rows], src.at[high, at_rows], x_send.at[k], x_recv.at[k], to_xp)
        c.start()
        return c

    swaps[2].start()
    beside[0].wait_recv()
    over_layers(along_z_half(rows))
    hear(0)
    tell(1)
    swaps[0].wait_recv()
    rims = [rim(orb, 0, False, rows_other)]
    swaps[1].wait_recv()
    rims.append(rim(orb, 1, True, rows_other))
    swaps[2].wait_recv()
    beside.append(to_mate(1, orb.at[mid, rows_other], zo.at[:, rows_other]))
    over_layers(along_y(orb))
    hear(1)
    tell(2)
    beside[1].wait_recv()
    over_layers(along_z_half(rows_other))
    given.wait_recv()
    for c in direct + rims:
        c.wait_recv()

    def by_edges(body, src, k):
        over_layers(body, 0, 6)
        sent = [rim(src, k, False)]
        over_layers(body, 10, 6)
        sent.append(rim(src, k + 1, True))
        over_layers(body, 6, 4)
        beside.append(to_mate(k // 2 + 1, src.at[mid], zf if k == 2 else zs))
        return sent

    def last_first(k):
        here = orb[k + 6]
        h = acc[k] + hf[k] + part_x(orb, k + 6) + (pot[k] - filter_center) * here
        first[k + 6] = h * (1.0 / filter_half)

    rims += by_edges(last_first, first, 2)

    hear(2)
    tell(3)
    over_layers(along_y(first))
    hear(3)
    tell(4)
    beside[2].wait_recv()
    over_layers(along_z(first, zf))
    hear(4)
    tell(5)
    for c in rims[2:]:
        c.wait_recv()

    def last_filtered(k):
        here = first[k + 6]
        h = acc[k] + part_x(first, k + 6) + (pot[k] - filter_center) * here
        fil[k + 6] = h * (2.0 / filter_half) - orb[k + 6]

    rims += by_edges(last_filtered, fil, 4)

    others = []
    for k in range(8):
        py = (y + far_first(k, 4)) % 8
        others.append((py // 2, x * 4 + (py % 2) * 2 + core, py // 4, pl.multiple_of((py % 4) * 8, 8)))

    def send_tiles(src, skip, got, which, pz, count=8):
        for py_hi, pdomain, half, row in others[:count]:
            rdma(
                src.at[skip + pz * 2 + half, pl.ds(row, 8)], got.at[zy],
                a2a_send.at[which], a2a_recv.at[which], (pz * 4 + py_hi, pdomain),
            ).start()

    def keep_tile(src, skip, got):
        got[zy] = src[skip + zy // 4, pl.ds(others[7][3], 8)]

    def all_tiles(got, which):
        return rdma(got.at[pl.ds(0, 63)], got.at[pl.ds(0, 63)], a2a_send.at[which], a2a_recv.at[which], mate)

    def filtered_out(i, _):
        send_tiles(fil, 6, gf, 0, (z + far_first(i, 4)) % 8)
        for j in (2 * i, 2 * i + 1):
            acc[j] = part_y(fil[j + 6])
        return 0

    lax.fori_loop(0, 7, filtered_out, 0)
    send_tiles(fil, 6, gf, 0, z, 7)
    keep_tile(fil, 6, gf)
    for j in (14, 15):
        acc[j] = part_y(fil[j + 6])
    hear(5)
    tell(6)

    beside[3].wait_recv()
    over_layers(along_z(fil, zs))
    hear(6)
    tell(7)
    for c in rims[4:]:
        c.wait_recv()

    def applied_layers(pz):
        for k in (2 * pz, 2 * pz + 1):
            hf[k] = acc[k] + part_x(fil, k + 6) + pot[k] * fil[k + 6]

    def applied_out(i, _):
        pz = (z + far_first(i, 4)) % 8
        applied_layers(pz)
        send_tiles(hf, 0, gh, 1, pz)
        return 0

    lax.fori_loop(0, 7, applied_out, 0)
    applied_layers(z)
    send_tiles(hf, 0, gh, 1, z, 7)
    keep_tile(hf, 0, gh)

    def contract(left, right):
        return lax.dot_general(left, right, (((1,), (1,)), ((), ())), preferred_element_type=jnp.float32)

    def halves(value):
        upper = value.astype(jnp.bfloat16)
        return upper, (value - upper.astype(jnp.float32)).astype(jnp.bfloat16)

    def cells(got, s):
        return jnp.concatenate([got[:, 2 * s, :], got[:, 2 * s + 1, :]], axis=1)

    hear(7)
    all_tiles(gf, 0).wait_recv()
    over = jnp.zeros((NB, NB), jnp.float32)
    for s in range(4):
        upper, lower = halves(cells(gf, s))
        g_high[s] = upper
        g_low[s] = lower
        over = over + (contract(upper, upper) + (contract(upper, lower) + contract(lower, upper)))
    part[:, :, :NB] = over.reshape(8, 8, NB)
    all_tiles(gh, 1).wait_recv()
    proj = jnp.zeros((NB, NB), jnp.float32)
    for s in range(4):
        upper, lower = halves(cells(gh, s))
        proj = proj + (contract(g_high[s], upper) + (contract(g_high[s], lower) + contract(g_low[s], upper)))
    part[:, :, NB:] = proj.reshape(8, 8, NB)

    slot = z * 2 + yl

    sides = [x * 4 + (1 - yl) * 2 + core, domain]
    for i in range(8):
        pz = (z + far_first(i, 4)) % 8
        for to in sides[: 2 if i < 7 else 1]:
            rdma(part.at[pz], r1.at[slot], red_send.at[0], red_recv.at[0], (pz * 4 + yh, to)).start()
    back = rdma(fil.at[mid, rows_other], out_f.at[yl], back_send, back_recv, at(z, yo, x, core))
    back.start()
    keep = pltpu.make_async_copy(fil.at[mid, rows], out_f.at[yl], loc_sem.at[2])
    keep.start()
    r1[slot] = part[z]
    red1 = rdma(r1.at[pl.ds(0, 15)], r1.at[pl.ds(0, 15)], red_send.at[0], red_recv.at[0], mate)
    red1.wait_recv()

    total = jnp.sum(r1[...], axis=0)
    for i in range(4):
        tot[i] = total[2 * i : 2 * i + 2]
    slot2 = yh * 8 + x * 2 + core

    columns = [
        ((x + far_first(i, 2)) % 4) * 4 + yl * 2 + c for i in range(4) for c in (1 - core, core)
    ]
    for i in range(4):
        ph = (yh + far_first(i, 2)) % 4
        for to in columns[: 8 if i < 3 else 7]:
            rdma(tot.at[ph], r2.at[slot2], red_send.at[1], red_recv.at[1], (z * 4 + ph, to)).start()
    r2[slot2] = tot[yh]
    red2 = rdma(r2.at[pl.ds(0, 31)], r2.at[pl.ds(0, 31)], red_send.at[1], red_recv.at[1], mate)
    red2.wait_recv()
    result = jnp.sum(r2[...], axis=0) * (1.0 / NCELL)
    out_s[...] = result[:, :NB]
    out_p[...] = result[:, NB:]

    for c in swaps + direct + [given]:
        c.wait_send()
    for c in beside:
        c.wait_send()
    for c in rims:
        c.wait_send()
    all_tiles(gf, 0).wait_send()
    all_tiles(gh, 1).wait_send()
    red1.wait_send()
    red2.wait_send()
    keep.wait()
    back.wait()


def deliver(filtered, inter, proj, out_f, out_s, out_p, sem):
    copies = [
        pltpu.make_async_copy(src, dst, sem.at[i])
        for i, (src, dst) in enumerate(((filtered, out_f), (inter, out_s), (proj, out_p)))
    ]
    for c in copies:
        c.start()
    for c in copies:
        c.wait()


def shards(orbitals, potential):
    f32 = jnp.float32
    vmem = pltpu.VMEM
    dma = pltpu.SemaphoreType.DMA
    any_ = pl.BlockSpec(memory_space=pl.ANY)
    hbm = pl.BlockSpec(memory_space=pltpu.HBM)
    full = pl.BlockSpec(memory_space=pltpu.VMEM)
    filtered, inter, proj = pl.pallas_call(
        kernel,
        out_shape=(
            jax.ShapeDtypeStruct((2, CX, CY, CZ), f32),
            jax.ShapeDtypeStruct((2, NB), f32),
            jax.ShapeDtypeStruct((2, NB), f32),
        ),
        in_specs=[hbm, hbm],
        out_specs=(hbm, full, full),
        scratch_shapes=[
            vmem((CX + 12, NY, CZ), f32),
            vmem((CX, NY, CZ), f32),
            vmem((CX + 12, NY, CZ), f32),
            vmem((CX + 12, NY, CZ), f32),
            vmem((CX, NY, CZ), f32),
            vmem((CX, NY, CZ), f32),
            vmem((CX, NY, CZ), f32),
            vmem((CX, NY, CZ), f32),
            vmem((CX, NY, CZ), f32),
            vmem((NB, 8, CZ), f32),
            vmem((NB, 8, CZ), f32),
            vmem((4, NB, 2 * CZ), jnp.bfloat16),
            vmem((4, NB, 2 * CZ), jnp.bfloat16),
            vmem((8, 8, 2 * NB), f32),
            vmem((16, 8, 2 * NB), f32),
            vmem((32, 2, 2 * NB), f32),
            vmem((4, 2, 2 * NB), f32),
            dma((3,)), dma((6,)), dma((6,)), dma((4,)), dma((4,)), dma((6,)), dma((6,)),
            dma((2,)), dma((2,)), dma, dma, dma((2,)), dma((2,)),
            pltpu.SemaphoreType.REGULAR((8,)),
        ],
        compiler_params=pltpu.CompilerParams(
            collective_id=0, has_side_effects=True, vmem_limit_bytes=32 << 20
        ),
        name="chebyshev_step",
    )(
        pltpu.with_memory_space_constraint(orbitals.reshape(2, CX, CY, CZ), pltpu.HBM),
        pltpu.with_memory_space_constraint(potential.reshape(CX, CY, CZ), pltpu.HBM),
    )
    filtered, inter, proj = pl.pallas_call(
        deliver,
        out_shape=(
            jax.ShapeDtypeStruct((2, CX, CY, CZ), f32),
            jax.ShapeDtypeStruct((2, NB), f32),
            jax.ShapeDtypeStruct((2, NB), f32),
        ),
        in_specs=[any_, any_, any_],
        out_specs=(hbm, hbm, hbm),
        scratch_shapes=[dma((3,))],
        compiler_params=pltpu.CompilerParams(vmem_limit_bytes=32 << 20),
        name="deliver",
    )(filtered, inter, proj)
    return filtered[:, None], inter, proj


def solution(mesh):
    return jax.shard_map(
        shards,
        mesh=mesh,
        in_specs=(P("band", "domain", None, None, None), P("domain", None, None, None)),
        out_specs=(P("band", "domain", None, None, None), P("band", None), P("band", None)),
        check_vma=False,
    )
```

```python
import functools

import jax
import jax.numpy as jnp
from jax import lax
from jax.experimental import pallas as pl
from jax.experimental.pallas import tpu as pltpu
from jax.sharding import PartitionSpec as P

second_coeffs = (
    -5369.0 / 1800.0,
    12.0 / 7.0,
    -15.0 / 56.0,
    10.0 / 189.0,
    -1.0 / 112.0,
    2.0 / 1925.0,
    -1.0 / 16632.0,
)
filter_center = 6.5
filter_half = 5.5
reach = 6
MESH = pl.DeviceIdType.MESH

CX, CY, CZ = 16, 16, 128
NY = 32
NB = 64
NCELL = 524288


def part_y(here):
    total = (-1.5 * second_coeffs[0]) * here
    for s in range(1, reach + 1):
        pair = pltpu.roll(here, s, 0) + pltpu.roll(here, NY - s, 0)
        total = total + (-0.5 * second_coeffs[s]) * pair
    return total


def part_z(here, beside, lane):
    total = None
    for s in range(1, reach + 1):
        ahead = pltpu.roll(jnp.where(lane < s, beside, here), CZ - s, 1)
        behind = pltpu.roll(jnp.where(lane >= CZ - s, beside, here), s, 1)
        term = (-0.5 * second_coeffs[s]) * (ahead + behind)
        total = term if total is None else total + term
    return total


def part_x(src, j):
    total = None
    for s in range(1, reach + 1):
        term = (-0.5 * second_coeffs[s]) * (src[j + s] + src[j - s])
        total = term if total is None else total + term
    return total


def far_first(i, half):
    return half + ((i + 1) // 2) * (2 * (i % 2) - 1)


def kernel(
    orb_in, pot_in, out_f, out_s, out_p,
    orb, give, pot, first, fil, zo, zf, zs, acc, hf, gf, gh, g_high, g_low, part, r1, r2, both_cores, tot,
    loc_sem, in_send, in_recv, core_send, core_recv, x_send, x_recv,
    a2a_send, a2a_recv, back_send, back_recv, red_send, red_recv, ring,
):
    band = lax.axis_index("band")
    domain = lax.axis_index("domain")
    z, yh = band // 4, band % 4
    x, yl, core = domain // 4, (domain // 2) % 2, domain % 2
    y = yh * 2 + yl
    zy = z * 8 + y
    mine = pl.multiple_of(yl * CY, CY)
    other = pl.multiple_of((1 - yl) * CY, CY)

    def at(pz, py, px, pc):
        return (pz * 4 + py // 2, px * 4 + (py % 2) * 2 + pc)

    xn, xp = (x + 1) % 4, (x + 3) % 4
    yo = y + 1 - 2 * yl
    yq = (y + 7 + 2 * yl) % 8
    mate = at(z, y, x, 1 - core)
    to_xn, to_xp = at(z, y, xn, core), at(z, y, xp, core)

    def rdma(src, dst, send, recv, to):
        return pltpu.make_async_remote_copy(
            src_ref=src, dst_ref=dst, send_sem=send, recv_sem=recv,
            device_id=to, device_id_type=MESH,
        )

    mid = pl.ds(6, CX)
    low, high = pl.ds(0, 6), pl.ds(22, 6)
    rows = pl.ds(mine, CY)
    rows_other = pl.ds(other, CY)

    local = [
        pltpu.make_async_copy(orb_in.at[yl], orb.at[mid, rows], loc_sem.at[0]),
        pltpu.make_async_copy(orb_in.at[1 - yl], give, loc_sem.at[3]),
        pltpu.make_async_copy(pot_in, pot.at[:, rows], loc_sem.at[1]),
    ]
    for c in local:
        c.start()

    bar = pltpu.get_barrier_semaphore()
    up_z, down_z = at((z + 1) % 8, y, x, core), at((z + 7) % 8, y, x, core)
    up_y, down_y = at(z, (y + 1) % 8, x, core), at(z, (y + 7) % 8, x, core)
    for to in (up_y, down_y, to_xn, to_xp, up_z, down_z, mate):
        pl.semaphore_signal(bar, inc=1, device_id=to, device_id_type=MESH)
    pl.semaphore_wait(bar, 7)
    for c in local:
        c.wait()

    far_z = (at((z + 2) % 8, y, x, core), at((z + 6) % 8, y, x, core))
    far_y = (at(z, (y + 2) % 8, x, core), at(z, (y + 6) % 8, x, core))
    words = (
        (up_z, down_z), far_z, (up_y, down_y), (up_y, down_y), far_y, (mate,), (to_xn, to_xp), (to_xn, to_xp),
    )

    def tell(k):
        for to in words[k]:
            pl.semaphore_signal(ring.at[k], inc=1, device_id=to, device_id_type=MESH)

    def hear(k):
        pl.semaphore_wait(ring.at[k], len(words[k]))

    swaps = [
        rdma(
            give.at[pl.ds(k, n)], orb.at[pl.ds(k + 6, n), rows],
            in_send.at[i], in_recv.at[i], at(z, yo, x, core),
        )
        for i, (k, n) in enumerate(((0, 6), (10, 6), (6, 4)))
    ]
    direct = [
        rdma(orb.at[pl.ds(16, 6), rows], orb.at[low, rows], in_send.at[3], in_recv.at[3], to_xn),
        rdma(orb.at[pl.ds(6, 6), rows], orb.at[high, rows], in_send.at[4], in_recv.at[4], to_xp),
    ]
    given = rdma(pot.at[:, rows], pot.at[:, rows], in_send.at[5], in_recv.at[5], at(z, yq, x, core))

    def to_mate(k, src, dst):
        c = rdma(src, dst, core_send.at[k], core_recv.at[k], mate)
        c.start()
        return c

    for c in swaps[:2] + direct + [given]:
        c.start()
    beside = [to_mate(0, orb.at[mid, rows], zo.at[:, rows])]
    tell(0)

    lane = lax.broadcasted_iota(jnp.int32, (NY, CZ), 1)
    lane_half = lax.broadcasted_iota(jnp.int32, (CY, CZ), 1)

    def over_layers(body, first_layer=0, count=CX):
        def step(k, _):
            body(k)
            return 0

        lax.fori_loop(first_layer, first_layer + count, step, 0)

    def along_y(src):
        def body(k):
            acc[k] = part_y(src[k + 6])

        return body

    def along_z(src, beside_src):
        def body(k):
            acc[k] = acc[k] + part_z(src[k + 6], beside_src[k], lane)

        return body

    def along_z_half(at_rows):
        def body(k):
            hf[k, at_rows] = part_z(orb[k + 6, at_rows], zo[k, at_rows], lane_half)

        return body

    def rim(src, k, to_next, at_rows=slice(None)):
        if to_next:
            c = rdma(src.at[pl.ds(16, 6), at_rows], src.at[low, at_rows], x_send.at[k], x_recv.at[k], to_xn)
        else:
            c = rdma(src.at[pl.ds(6, 6), at_rows], src.at[high, at_rows], x_send.at[k], x_recv.at[k], to_xp)
        c.start()
        return c

    swaps[2].start()
    beside[0].wait_recv()
    over_layers(along_z_half(rows))
    hear(0)
    tell(1)
    swaps[0].wait_recv()
    rims = [rim(orb, 0, False, rows_other)]
    swaps[1].wait_recv()
    rims.append(rim(orb, 1, True, rows_other))
    swaps[2].wait_recv()
    beside.append(to_mate(1, orb.at[mid, rows_other], zo.at[:, rows_other]))
    over_layers(along_y(orb))
    hear(1)
    tell(2)
    beside[1].wait_recv()
    over_layers(along_z_half(rows_other))
    given.wait_recv()

    def inner(body):
        over_layers(body, 6, 4)

    def edges(body, src, k):
        over_layers(body, 0, 6)
        sent = [rim(src, k, False)]
        over_layers(body, 10, 6)
        sent.append(rim(src, k + 1, True))
        beside.append(to_mate(k // 2 + 1, src.at[mid], zf if k == 2 else zs))
        return sent

    def last_first(k):
        here = orb[k + 6]
        h = acc[k] + hf[k] + part_x(orb, k + 6) + (pot[k] - filter_center) * here
        first[k + 6] = h * (1.0 / filter_half)

    inner(last_first)
    for c in direct + rims:
        c.wait_recv()
    rims += edges(last_first, first, 2)

    hear(2)
    tell(3)
    over_layers(along_y(first))
    hear(3)
    tell(4)
    beside[2].wait_recv()
    over_layers(along_z(first, zf))
    hear(4)
    tell(5)

    def layer_of(group, pz):
        m = pz // 2
        return (6 + m, m, 4 + m + 4 * (m // 2), 12 + m)[group]

    def send_tiles(src, skip, got, which, pz, groups, at_home=False):
        for group in groups:
            for b in range(2):
                py = (pz + group + 4 * b) % 8
                row = pl.multiple_of(16 * b + 8 * (pz % 2), 8)
                copy = rdma(
                    src.at[skip + layer_of(group, pz), pl.ds(row, 8)], got.at[zy],
                    a2a_send.at[which], a2a_recv.at[which], at(pz, py, x, core),
                )
                if at_home:
                    pl.when(py != y)(copy.start)
                else:
                    copy.start()

    def all_tiles(got, which):
        return rdma(got.at[pl.ds(0, 63)], got.at[pl.ds(0, 63)], a2a_send.at[which], a2a_recv.at[which], mate)

    def send_inner(src, skip, got, which):
        def turn(i, _):
            send_tiles(src, skip, got, which, (z + far_first(i, 4)) % 8, (0,))
            return 0

        lax.fori_loop(0, 7, turn, 0)
        send_tiles(src, skip, got, which, z, (0,), True)

    def keep_tile(src, skip, got):
        group, b = (y + 8 - z) % 4, ((y + 8 - z) % 8) // 4
        row = pl.multiple_of(16 * b + 8 * (z % 2), 8)
        for k in range(4):
            @pl.when(group == k)
            def _():
                got[zy] = src[skip + layer_of(k, z), pl.ds(row, 8)]

    def last_filtered(k):
        here = first[k + 6]
        h = acc[k] + part_x(first, k + 6) + (pot[k] - filter_center) * here
        fil[k + 6] = h * (2.0 / filter_half) - orb[k + 6]

    inner(last_filtered)
    send_inner(fil, 6, gf, 0)
    for c in rims[2:4]:
        c.wait_recv()
    rims += edges(last_filtered, fil, 4)

    def filtered_out(i, _):
        send_tiles(fil, 6, gf, 0, (z + far_first(i, 4)) % 8, (1, 2, 3))
        for j in (2 * i, 2 * i + 1):
            acc[j] = part_y(fil[j + 6])
        return 0

    lax.fori_loop(0, 7, filtered_out, 0)
    send_tiles(fil, 6, gf, 0, z, (1, 2, 3), True)
    keep_tile(fil, 6, gf)
    for j in (14, 15):
        acc[j] = part_y(fil[j + 6])
    hear(5)
    tell(6)

    def applied_layer(k):
        hf[k] = acc[k] + part_x(fil, k + 6) + pot[k] * fil[k + 6]

    beside[3].wait_recv()
    over_layers(along_z(fil, zs))
    hear(6)
    tell(7)
    inner(applied_layer)
    send_inner(hf, 0, gh, 1)
    for c in rims[4:]:
        c.wait_recv()
    over_layers(applied_layer, 0, 6)
    over_layers(applied_layer, 10, 6)

    def applied_out(i, _):
        send_tiles(hf, 0, gh, 1, (z + far_first(i, 4)) % 8, (1, 2, 3))
        return 0

    lax.fori_loop(0, 7, applied_out, 0)
    send_tiles(hf, 0, gh, 1, z, (1, 2, 3), True)
    keep_tile(hf, 0, gh)

    def contract(left, right):
        return lax.dot_general(left, right, (((1,), (1,)), ((), ())), preferred_element_type=jnp.float32)

    def halves(value):
        upper = value.astype(jnp.bfloat16)
        return upper, (value - upper.astype(jnp.float32)).astype(jnp.bfloat16)

    def cells(got, s):
        return jnp.concatenate([got[:, 2 * s, :], got[:, 2 * s + 1, :]], axis=1)

    hear(7)
    all_tiles(gf, 0).wait_recv()
    over = jnp.zeros((NB, NB), jnp.float32)
    for s in range(4):
        upper, lower = halves(cells(gf, s))
        g_high[s] = upper
        g_low[s] = lower
        over = over + (contract(upper, upper) + (contract(upper, lower) + contract(lower, upper)))
    part[:, :, :NB] = over.reshape(8, 8, NB)
    all_tiles(gh, 1).wait_recv()
    proj = jnp.zeros((NB, NB), jnp.float32)
    for s in range(4):
        upper, lower = halves(cells(gh, s))
        proj = proj + (contract(g_high[s], upper) + (contract(g_high[s], lower) + contract(g_low[s], upper)))
    part[:, :, NB:] = proj.reshape(8, 8, NB)

    slot = z * 2 + yl

    sides = [x * 4 + (1 - yl) * 2 + core, domain]
    for i in range(8):
        pz = (z + far_first(i, 4)) % 8
        for to in sides[: 2 if i < 7 else 1]:
            rdma(part.at[pz], r1.at[slot], red_send.at[0], red_recv.at[0], (pz * 4 + yh, to)).start()
    back = rdma(fil.at[mid, rows_other], out_f.at[yl], back_send, back_recv, at(z, yo, x, core))
    back.start()
    keep = pltpu.make_async_copy(fil.at[mid, rows], out_f.at[yl], loc_sem.at[2])
    keep.start()
    r1[slot] = part[z]
    red1 = rdma(r1.at[pl.ds(0, 15)], r1.at[pl.ds(0, 15)], red_send.at[0], red_recv.at[0], mate)
    red1.wait_recv()

    both_cores[0] = jnp.sum(r1[...], axis=0)
    red3 = rdma(both_cores.at[0], both_cores.at[1], red_send.at[2], red_recv.at[2], mate)
    red3.start()
    red3.wait_recv()
    total = both_cores[0] + both_cores[1]
    for i in range(4):
        tot[i] = total[2 * i : 2 * i + 2]
    slot2 = yh * 4 + x
    columns = [((x + far_first(i, 2)) % 4) * 4 + yl * 2 + core for i in range(4)]
    for i in range(4):
        ph = (yh + far_first(i, 2)) % 4
        for to in columns[: 4 if i < 3 else 3]:
            rdma(tot.at[ph], r2.at[slot2], red_send.at[1], red_recv.at[1], (z * 4 + ph, to)).start()
    r2[slot2] = tot[yh]
    red2 = rdma(r2.at[pl.ds(0, 15)], r2.at[pl.ds(0, 15)], red_send.at[1], red_recv.at[1], mate)
    red2.wait_recv()
    result = jnp.sum(r2[...], axis=0) * (1.0 / NCELL)
    out_s[...] = result[:, :NB]
    out_p[...] = result[:, NB:]

    for c in swaps + direct + [given]:
        c.wait_send()
    for c in beside:
        c.wait_send()
    for c in rims:
        c.wait_send()
    all_tiles(gf, 0).wait_send()
    all_tiles(gh, 1).wait_send()
    red1.wait_send()
    red2.wait_send()
    red3.wait_send()
    keep.wait()
    back.wait()


def deliver(filtered, inter, proj, out_f, out_s, out_p, sem):
    copies = [
        pltpu.make_async_copy(src, dst, sem.at[i])
        for i, (src, dst) in enumerate(((filtered, out_f), (inter, out_s), (proj, out_p)))
    ]
    for c in copies:
        c.start()
    for c in copies:
        c.wait()


def shards(orbitals, potential):
    f32 = jnp.float32
    vmem = pltpu.VMEM
    dma = pltpu.SemaphoreType.DMA
    any_ = pl.BlockSpec(memory_space=pl.ANY)
    hbm = pl.BlockSpec(memory_space=pltpu.HBM)
    full = pl.BlockSpec(memory_space=pltpu.VMEM)
    filtered, inter, proj = pl.pallas_call(
        kernel,
        out_shape=(
            jax.ShapeDtypeStruct((2, CX, CY, CZ), f32),
            jax.ShapeDtypeStruct((2, NB), f32),
            jax.ShapeDtypeStruct((2, NB), f32),
        ),
        in_specs=[hbm, hbm],
        out_specs=(hbm, full, full),
        scratch_shapes=[
            vmem((CX + 12, NY, CZ), f32),
            vmem((CX, CY, CZ), f32),
            vmem((CX, NY, CZ), f32),
            vmem((CX + 12, NY, CZ), f32),
            vmem((CX + 12, NY, CZ), f32),
            vmem((CX, NY, CZ), f32),
            vmem((CX, NY, CZ), f32),
            vmem((CX, NY, CZ), f32),
            vmem((CX, NY, CZ), f32),
            vmem((CX, NY, CZ), f32),
            vmem((NB, 8, CZ), f32),
            vmem((NB, 8, CZ), f32),
            vmem((4, NB, 2 * CZ), jnp.bfloat16),
            vmem((4, NB, 2 * CZ), jnp.bfloat16),
            vmem((8, 8, 2 * NB), f32),
            vmem((16, 8, 2 * NB), f32),
            vmem((16, 2, 2 * NB), f32),
            vmem((2, 8, 2 * NB), f32),
            vmem((4, 2, 2 * NB), f32),
            dma((4,)), dma((6,)), dma((6,)), dma((4,)), dma((4,)), dma((6,)), dma((6,)),
            dma((2,)), dma((2,)), dma, dma, dma((3,)), dma((3,)),
            pltpu.SemaphoreType.REGULAR((8,)),
        ],
        compiler_params=pltpu.CompilerParams(
            collective_id=0, has_side_effects=True, vmem_limit_bytes=32 << 20
        ),
        name="chebyshev_step",
    )(
        pltpu.with_memory_space_constraint(orbitals.reshape(2, CX, CY, CZ), pltpu.HBM),
        pltpu.with_memory_space_constraint(potential.reshape(CX, CY, CZ), pltpu.HBM),
    )
    filtered, inter, proj = pl.pallas_call(
        deliver,
        out_shape=(
            jax.ShapeDtypeStruct((2, CX, CY, CZ), f32),
            jax.ShapeDtypeStruct((2, NB), f32),
            jax.ShapeDtypeStruct((2, NB), f32),
        ),
        in_specs=[any_, any_, any_],
        out_specs=(hbm, hbm, hbm),
        scratch_shapes=[dma((3,))],
        compiler_params=pltpu.CompilerParams(vmem_limit_bytes=32 << 20),
        name="deliver",
    )(filtered, inter, proj)
    return filtered[:, None], inter, proj


def solution(mesh):
    return jax.shard_map(
        shards,
        mesh=mesh,
        in_specs=(P("band", "domain", None, None, None), P("domain", None, None, None)),
        out_specs=(P("band", "domain", None, None, None), P("band", None), P("band", None)),
        check_vma=False,
    )
```

```python
import functools

import jax
import jax.numpy as jnp
from jax import lax
from jax.experimental import pallas as pl
from jax.experimental.pallas import tpu as pltpu
from jax.sharding import PartitionSpec as P

second_coeffs = (
    -5369.0 / 1800.0,
    12.0 / 7.0,
    -15.0 / 56.0,
    10.0 / 189.0,
    -1.0 / 112.0,
    2.0 / 1925.0,
    -1.0 / 16632.0,
)
filter_center = 6.5
filter_half = 5.5
reach = 6
MESH = pl.DeviceIdType.MESH

CX, CY, CZ = 16, 16, 128
NY = 32
NB = 64
NCELL = 524288


def part_y(here):
    total = (-1.5 * second_coeffs[0]) * here
    for s in range(1, reach + 1):
        pair = pltpu.roll(here, s, 0) + pltpu.roll(here, NY - s, 0)
        total = total + (-0.5 * second_coeffs[s]) * pair
    return total


def part_z(here, beside, lane):
    total = None
    for s in range(1, reach + 1):
        ahead = pltpu.roll(jnp.where(lane < s, beside, here), CZ - s, 1)
        behind = pltpu.roll(jnp.where(lane >= CZ - s, beside, here), s, 1)
        term = (-0.5 * second_coeffs[s]) * (ahead + behind)
        total = term if total is None else total + term
    return total


def part_x(src, j):
    total = None
    for s in range(1, reach + 1):
        term = (-0.5 * second_coeffs[s]) * (src[j + s] + src[j - s])
        total = term if total is None else total + term
    return total


def far_first(i, half):
    return half + ((i + 1) // 2) * (2 * (i % 2) - 1)


def kernel(
    orb_in, pot_in, out_f, out_s, out_p,
    orb, give, pot, first, fil, zo, zf, zs, acc, along, hf, gf, gh, g_high, g_low, part, r1, r2, tot,
    loc_sem, in_send, in_recv, core_send, core_recv, x_send, x_recv,
    a2a_send, a2a_recv, back_send, back_recv, red_send, red_recv, ring,
):
    band = lax.axis_index("band")
    domain = lax.axis_index("domain")
    z, yh = band // 4, band % 4
    x, yl, core = domain // 4, (domain // 2) % 2, domain % 2
    y = yh * 2 + yl
    zy = z * 8 + y
    mine = pl.multiple_of(yl * CY, CY)
    other = pl.multiple_of((1 - yl) * CY, CY)

    def at(pz, py, px, pc):
        return (pz * 4 + py // 2, px * 4 + (py % 2) * 2 + pc)

    xn, xp = (x + 1) % 4, (x + 3) % 4
    yo = y + 1 - 2 * yl
    yq = (y + 7 + 2 * yl) % 8
    mate = at(z, y, x, 1 - core)
    to_xn, to_xp = at(z, y, xn, core), at(z, y, xp, core)

    def rdma(src, dst, send, recv, to):
        return pltpu.make_async_remote_copy(
            src_ref=src, dst_ref=dst, send_sem=send, recv_sem=recv,
            device_id=to, device_id_type=MESH,
        )

    mid = pl.ds(6, CX)
    low, high = pl.ds(0, 6), pl.ds(22, 6)
    rows = pl.ds(mine, CY)
    rows_other = pl.ds(other, CY)

    local = [
        pltpu.make_async_copy(orb_in.at[yl], orb.at[pl.ds(12, CX), rows], loc_sem.at[0]),
        pltpu.make_async_copy(orb_in.at[1 - yl], give, loc_sem.at[3]),
        pltpu.make_async_copy(pot_in, pot.at[mid, rows], loc_sem.at[1]),
    ]
    for c in local:
        c.start()

    bar = pltpu.get_barrier_semaphore()
    up_z, down_z = at((z + 1) % 8, y, x, core), at((z + 7) % 8, y, x, core)
    up_y, down_y = at(z, (y + 1) % 8, x, core), at(z, (y + 7) % 8, x, core)
    across = [at(z, yq, xn, core), at(z, yq, xp, core)]
    for to in (up_y, down_y, to_xn, to_xp, up_z, down_z, mate, *across):
        pl.semaphore_signal(bar, inc=1, device_id=to, device_id_type=MESH)
    pl.semaphore_wait(bar, 9)
    for c in local:
        c.wait()

    far_z = (at((z + 2) % 8, y, x, core), at((z + 6) % 8, y, x, core))
    far_y = (at(z, (y + 2) % 8, x, core), at(z, (y + 6) % 8, x, core))
    words = (
        (up_z, down_z), far_z, (up_y, down_y), (up_y, down_y), far_y, (mate,), (to_xn, to_xp), (to_xn, to_xp),
    )

    def tell(k):
        for to in words[k]:
            pl.semaphore_signal(ring.at[k], inc=1, device_id=to, device_id_type=MESH)

    def hear(k):
        pl.semaphore_wait(ring.at[k], len(words[k]))

    def entry(k, src, dst, to):
        return rdma(src, dst, in_send.at[k], in_recv.at[k], to)

    swaps = [
        entry(0, give.at[pl.ds(0, 8)], orb.at[pl.ds(12, 8), rows], at(z, yo, x, core)),
        entry(1, give.at[pl.ds(8, 8)], orb.at[pl.ds(20, 8), rows], at(z, yo, x, core)),
    ]
    direct = [
        entry(2, orb.at[pl.ds(16, 12), rows], orb.at[pl.ds(0, 12), rows], to_xn),
        entry(3, orb.at[pl.ds(12, 12), rows], orb.at[pl.ds(28, 12), rows], to_xp),
    ]
    given = [
        entry(4, pot.at[mid, rows], pot.at[mid, rows], at(z, yq, x, core)),
        entry(5, pot.at[pl.ds(16, 6), rows], pot.at[low, rows], to_xn),
        entry(6, pot.at[pl.ds(6, 6), rows], pot.at[high, rows], to_xp),
        entry(7, pot.at[pl.ds(16, 6), rows], pot.at[low, rows], across[0]),
        entry(8, pot.at[pl.ds(6, 6), rows], pot.at[high, rows], across[1]),
    ]

    def to_mate(k, src, dst):
        c = rdma(src, dst, core_send.at[k], core_recv.at[k], mate)
        c.start()
        return c

    for c in swaps + direct + given:
        c.start()
    beside = [to_mate(0, orb.at[pl.ds(12, CX), rows], zo.at[mid, rows])]
    tell(0)

    lane = lax.broadcasted_iota(jnp.int32, (NY, CZ), 1)
    lane_half = lax.broadcasted_iota(jnp.int32, (CY, CZ), 1)

    def over_layers(body, first_layer=0, count=CX):
        def step(k, _):
            body(k)
            return 0

        lax.fori_loop(first_layer, first_layer + count, step, 0)

    def halo_layers(body):
        over_layers(body, 0, 6)
        over_layers(body, 22, 6)

    def orb_along_y(k):
        acc[k] = part_y(orb[k + 6])

    def orb_along_z(at_rows):
        def body(k):
            along[k, at_rows] = part_z(orb[k + 6, at_rows], zo[k, at_rows], lane_half)

        return body

    def orb_along_x(k):
        h = acc[k] + along[k] + part_x(orb, k + 6) + (pot[k] - filter_center) * orb[k + 6]
        first[k] = h * (1.0 / filter_half)

    def along_y(src):
        def body(k):
            acc[k] = part_y(src[k + 6])

        return body

    def along_z(src, beside_src):
        def body(k):
            acc[k] = acc[k] + part_z(src[k + 6], beside_src[k], lane)

        return body

    def forward(k, start, count, to, dst):
        c = rdma(
            orb.at[pl.ds(start, count), rows_other], orb.at[pl.ds(dst, count), rows_other],
            x_send.at[k], x_recv.at[k], to,
        )
        c.start()
        return c

    beside[0].wait_recv()
    over_layers(orb_along_z(rows), 6)
    hear(0)
    tell(1)
    swaps[0].wait_recv()
    rims = [forward(0, 12, 8, to_xp, 28), forward(1, 16, 4, to_xn, 0)]
    swaps[1].wait_recv()
    rims += [forward(2, 20, 4, to_xp, 36), forward(3, 20, 8, to_xn, 4)]
    beside.append(to_mate(1, orb.at[pl.ds(12, CX), rows_other], zo.at[mid, rows_other]))
    for c in direct:
        c.wait_recv()
    beside.append(to_mate(2, orb.at[pl.ds(6, 6), rows], zo.at[low, rows]))
    beside.append(to_mate(3, orb.at[pl.ds(28, 6), rows], zo.at[high, rows]))
    over_layers(orb_along_y, 6)
    hear(1)
    tell(2)
    beside[1].wait_recv()
    over_layers(orb_along_z(rows_other), 6)
    beside[2].wait_recv()
    beside[3].wait_recv()
    halo_layers(orb_along_z(rows))
    given[0].wait_recv()
    over_layers(orb_along_x, 12, 4)
    for c in rims:
        c.wait_recv()
    beside.append(to_mate(4, orb.at[pl.ds(6, 6), rows_other], zo.at[low, rows_other]))
    beside.append(to_mate(5, orb.at[pl.ds(28, 6), rows_other], zo.at[high, rows_other]))
    over_layers(orb_along_x, 6, 6)
    over_layers(orb_along_x, 16, 6)
    beside.append(to_mate(6, first.at[mid], zf))
    halo_layers(orb_along_y)
    hear(2)
    tell(3)
    for c in given[1:]:
        c.wait_recv()
    beside[4].wait_recv()
    beside[5].wait_recv()
    halo_layers(orb_along_z(rows_other))
    halo_layers(orb_along_x)

    over_layers(along_y(first))
    hear(3)
    tell(4)
    beside[6].wait_recv()
    over_layers(along_z(first, zf))
    hear(4)
    tell(5)

    def last_filtered(k):
        here = first[k + 6]
        h = acc[k] + part_x(first, k + 6) + (pot[k + 6] - filter_center) * here
        fil[k + 6] = h * (2.0 / filter_half) - orb[k + 12]

    def rim(k, start, dst, to):
        c = rdma(fil.at[pl.ds(start, 6)], fil.at[dst], x_send.at[k], x_recv.at[k], to)
        c.start()
        return c

    over_layers(last_filtered, 0, 6)
    rims.append(rim(4, 6, high, to_xp))
    over_layers(last_filtered, 10, 6)
    rims.append(rim(5, 16, low, to_xn))
    over_layers(last_filtered, 6, 4)
    beside.append(to_mate(7, fil.at[mid], zs))

    def layer_of(group, pz):
        m = pz // 2
        return (6 + m, m, 4 + m + 4 * (m // 2), 12 + m)[group]

    def send_tiles(src, skip, got, which, pz, groups, at_home=False):
        for group in groups:
            for b in range(2):
                py = (pz + group + 4 * b) % 8
                row = pl.multiple_of(16 * b + 8 * (pz % 2), 8)
                copy = rdma(
                    src.at[skip + layer_of(group, pz), pl.ds(row, 8)], got.at[zy],
                    a2a_send.at[which], a2a_recv.at[which], at(pz, py, x, core),
                )
                if at_home:
                    pl.when(py != y)(copy.start)
                else:
                    copy.start()

    def all_tiles(got, which):
        return rdma(got.at[pl.ds(0, 63)], got.at[pl.ds(0, 63)], a2a_send.at[which], a2a_recv.at[which], mate)

    def send_inner(src, skip, got, which):
        def turn(i, _):
            send_tiles(src, skip, got, which, (z + far_first(i, 4)) % 8, (0,))
            return 0

        lax.fori_loop(0, 7, turn, 0)
        send_tiles(src, skip, got, which, z, (0,), True)

    def keep_tile(src, skip, got):
        group, b = (y + 8 - z) % 4, ((y + 8 - z) % 8) // 4
        row = pl.multiple_of(16 * b + 8 * (z % 2), 8)
        for k in range(4):
            @pl.when(group == k)
            def _():
                got[zy] = src[skip + layer_of(k, z), pl.ds(row, 8)]

    def filtered_out(i, _):
        send_tiles(fil, 6, gf, 0, (z + far_first(i, 4)) % 8, (0, 1, 2, 3))
        for j in (2 * i, 2 * i + 1):
            acc[j] = part_y(fil[j + 6])
        return 0

    lax.fori_loop(0, 7, filtered_out, 0)
    send_tiles(fil, 6, gf, 0, z, (0, 1, 2, 3), True)
    keep_tile(fil, 6, gf)
    for j in (14, 15):
        acc[j] = part_y(fil[j + 6])
    hear(5)
    tell(6)

    def applied_layer(k):
        hf[k] = acc[k] + part_x(fil, k + 6) + pot[k + 6] * fil[k + 6]

    beside[7].wait_recv()
    over_layers(along_z(fil, zs))
    hear(6)
    tell(7)
    over_layers(applied_layer, 6, 4)
    send_inner(hf, 0, gh, 1)
    for c in rims[4:]:
        c.wait_recv()
    over_layers(applied_layer, 0, 6)
    over_layers(applied_layer, 10, 6)

    def applied_out(i, _):
        send_tiles(hf, 0, gh, 1, (z + far_first(i, 4)) % 8, (1, 2, 3))
        return 0

    lax.fori_loop(0, 7, applied_out, 0)
    send_tiles(hf, 0, gh, 1, z, (1, 2, 3), True)
    keep_tile(hf, 0, gh)

    def contract(left, right):
        return lax.dot_general(left, right, (((1,), (1,)), ((), ())), preferred_element_type=jnp.float32)

    def halves(value):
        upper = value.astype(jnp.bfloat16)
        return upper, (value - upper.astype(jnp.float32)).astype(jnp.bfloat16)

    def cells(got, s):
        return jnp.concatenate([got[:, 2 * s, :], got[:, 2 * s + 1, :]], axis=1)

    hear(7)
    all_tiles(gf, 0).wait_recv()
    over = jnp.zeros((NB, NB), jnp.float32)
    for s in range(4):
        upper, lower = halves(cells(gf, s))
        g_high[s] = upper
        g_low[s] = lower
        over = over + (contract(upper, upper) + (contract(upper, lower) + contract(lower, upper)))
    part[:, :, :NB] = over.reshape(32, 2, NB)
    all_tiles(gh, 1).wait_recv()
    proj = jnp.zeros((NB, NB), jnp.float32)
    for s in range(4):
        upper, lower = halves(cells(gh, s))
        proj = proj + (contract(g_high[s], upper) + (contract(g_high[s], lower) + contract(g_low[s], upper)))
    part[:, :, NB:] = proj.reshape(32, 2, NB)

    def send_rows(pz, at_home=False):
        for k in range(8):
            py = (y + far_first(k, 4)) % 8
            if not (at_home and k == 7):
                rdma(
                    part.at[pz * 4 + py // 2], r1.at[zy], red_send.at[0], red_recv.at[0], at(pz, py, x, core)
                ).start()

    def rows_out(i, _):
        send_rows((z + far_first(i, 4)) % 8)
        return 0

    lax.fori_loop(0, 7, rows_out, 0)
    send_rows(z, True)
    r1[zy] = part[band]
    red1 = rdma(r1.at[pl.ds(0, 63)], r1.at[pl.ds(0, 63)], red_send.at[0], red_recv.at[0], mate)
    red1.wait_recv()
    back = rdma(fil.at[mid, rows_other], out_f.at[yl], back_send, back_recv, at(z, yo, x, core))
    back.start()
    keep = pltpu.make_async_copy(fil.at[mid, rows], out_f.at[yl], loc_sem.at[2])
    keep.start()

    tot[...] = jnp.sum(r1[...], axis=0)
    slot = x * 2 + core
    for i in range(4):
        for pc in (1 - core, core)[: 2 if i < 3 else 1]:
            to = at(z, y, (x + far_first(i, 2)) % 4, pc)
            rdma(tot, r2.at[slot], red_send.at[1], red_recv.at[1], to).start()
    r2[slot] = tot[...]
    red2 = rdma(r2.at[pl.ds(0, 7)], r2.at[pl.ds(0, 7)], red_send.at[1], red_recv.at[1], mate)
    red2.wait_recv()
    result = jnp.sum(r2[...], axis=0) * (1.0 / NCELL)
    out_s[...] = result[:, :NB]
    out_p[...] = result[:, NB:]

    for c in swaps + direct + given:
        c.wait_send()
    for c in beside:
        c.wait_send()
    for c in rims:
        c.wait_send()
    all_tiles(gf, 0).wait_send()
    all_tiles(gh, 1).wait_send()
    red1.wait_send()
    red2.wait_send()
    keep.wait()
    back.wait()


def deliver(filtered, inter, proj, out_f, out_s, out_p, sem):
    copies = [
        pltpu.make_async_copy(src, dst, sem.at[i])
        for i, (src, dst) in enumerate(((filtered, out_f), (inter, out_s), (proj, out_p)))
    ]
    for c in copies:
        c.start()
    for c in copies:
        c.wait()


def shards(orbitals, potential):
    f32 = jnp.float32
    vmem = pltpu.VMEM
    dma = pltpu.SemaphoreType.DMA
    any_ = pl.BlockSpec(memory_space=pl.ANY)
    hbm = pl.BlockSpec(memory_space=pltpu.HBM)
    full = pl.BlockSpec(memory_space=pltpu.VMEM)
    filtered, inter, proj = pl.pallas_call(
        kernel,
        out_shape=(
            jax.ShapeDtypeStruct((2, CX, CY, CZ), f32),
            jax.ShapeDtypeStruct((2, NB), f32),
            jax.ShapeDtypeStruct((2, NB), f32),
        ),
        in_specs=[hbm, hbm],
        out_specs=(hbm, full, full),
        scratch_shapes=[
            vmem((CX + 24, NY, CZ), f32),
            vmem((CX, CY, CZ), f32),
            vmem((CX + 12, NY, CZ), f32),
            vmem((CX + 12, NY, CZ), f32),
            vmem((CX + 12, NY, CZ), f32),
            vmem((CX + 12, NY, CZ), f32),
            vmem((CX, NY, CZ), f32),
            vmem((CX, NY, CZ), f32),
            vmem((CX + 12, NY, CZ), f32),
            vmem((CX + 12, NY, CZ), f32),
            vmem((CX, NY, CZ), f32),
            vmem((NB, 8, CZ), f32),
            vmem((NB, 8, CZ), f32),
            vmem((4, NB, 2 * CZ), jnp.bfloat16),
            vmem((4, NB, 2 * CZ), jnp.bfloat16),
            vmem((32, 2, 2 * NB), f32),
            vmem((64, 2, 2 * NB), f32),
            vmem((8, 2, 2 * NB), f32),
            vmem((2, 2 * NB), f32),
            dma((4,)), dma((9,)), dma((9,)), dma((8,)), dma((8,)), dma((6,)), dma((6,)),
            dma((2,)), dma((2,)), dma, dma, dma((2,)), dma((2,)),
            pltpu.SemaphoreType.REGULAR((8,)),
        ],
        compiler_params=pltpu.CompilerParams(
            collective_id=0, has_side_effects=True, vmem_limit_bytes=32 << 20
        ),
        name="chebyshev_step",
    )(
        pltpu.with_memory_space_constraint(orbitals.reshape(2, CX, CY, CZ), pltpu.HBM),
        pltpu.with_memory_space_constraint(potential.reshape(CX, CY, CZ), pltpu.HBM),
    )
    filtered, inter, proj = pl.pallas_call(
        deliver,
        out_shape=(
            jax.ShapeDtypeStruct((2, CX, CY, CZ), f32),
            jax.ShapeDtypeStruct((2, NB), f32),
            jax.ShapeDtypeStruct((2, NB), f32),
        ),
        in_specs=[any_, any_, any_],
        out_specs=(hbm, hbm, hbm),
        scratch_shapes=[dma((3,))],
        compiler_params=pltpu.CompilerParams(vmem_limit_bytes=32 << 20),
        name="deliver",
    )(filtered, inter, proj)
    return filtered[:, None], inter, proj


def solution(mesh):
    return jax.shard_map(
        shards,
        mesh=mesh,
        in_specs=(P("band", "domain", None, None, None), P("domain", None, None, None)),
        out_specs=(P("band", "domain", None, None, None), P("band", None), P("band", None)),
        check_vma=False,
    )
```

```python
import functools

import jax
import jax.numpy as jnp
from jax import lax
from jax.experimental import pallas as pl
from jax.experimental.pallas import tpu as pltpu
from jax.sharding import PartitionSpec as P

second_coeffs = (
    -5369.0 / 1800.0,
    12.0 / 7.0,
    -15.0 / 56.0,
    10.0 / 189.0,
    -1.0 / 112.0,
    2.0 / 1925.0,
    -1.0 / 16632.0,
)
filter_center = 6.5
filter_half = 5.5
reach = 6
MESH = pl.DeviceIdType.MESH

CX, CY, CZ = 16, 16, 128
NY = 32
NB = 64
NCELL = 524288


def part_y(here):
    total = (-1.5 * second_coeffs[0]) * here
    for s in range(1, reach + 1):
        pair = pltpu.roll(here, s, 0) + pltpu.roll(here, NY - s, 0)
        total = total + (-0.5 * second_coeffs[s]) * pair
    return total


def part_z(here, beside, lane):
    total = None
    for s in range(1, reach + 1):
        ahead = pltpu.roll(jnp.where(lane < s, beside, here), CZ - s, 1)
        behind = pltpu.roll(jnp.where(lane >= CZ - s, beside, here), s, 1)
        term = (-0.5 * second_coeffs[s]) * (ahead + behind)
        total = term if total is None else total + term
    return total


def far_first(i, half):
    return half + ((i + 1) // 2) * (2 * (i % 2) - 1)


def kernel(
    orb_in, pot_in, out_f, out_s, out_p,
    orb, give, pot, first, fil, zo, zf, zs, acc, hf, gf, gh, g_high, g_low, part, r1, r2, tot,
    loc_sem, in_send, in_recv, core_send, core_recv, x_send, x_recv,
    a2a_send, a2a_recv, back_send, back_recv, red_send, red_recv, ring,
):
    band = lax.axis_index("band")
    domain = lax.axis_index("domain")
    z, yh = band // 4, band % 4
    x, yl, core = domain // 4, (domain // 2) % 2, domain % 2
    y = yh * 2 + yl
    zy = z * 8 + y
    mine = pl.multiple_of(yl * CY, CY)
    other = pl.multiple_of((1 - yl) * CY, CY)

    def at(pz, py, px, pc):
        return (pz * 4 + py // 2, px * 4 + (py % 2) * 2 + pc)

    xn, xp = (x + 1) % 4, (x + 3) % 4
    yo = y + 1 - 2 * yl
    yq = (y + 7 + 2 * yl) % 8
    mate = at(z, y, x, 1 - core)
    to_xn, to_xp = at(z, y, xn, core), at(z, y, xp, core)

    def rdma(src, dst, send, recv, to):
        return pltpu.make_async_remote_copy(
            src_ref=src, dst_ref=dst, send_sem=send, recv_sem=recv,
            device_id=to, device_id_type=MESH,
        )

    mid = pl.ds(6, CX)
    low, high = pl.ds(0, 6), pl.ds(22, 6)
    rows = pl.ds(mine, CY)
    rows_other = pl.ds(other, CY)

    local = [
        pltpu.make_async_copy(orb_in.at[yl], orb.at[mid, rows], loc_sem.at[0]),
        pltpu.make_async_copy(orb_in.at[1 - yl], give, loc_sem.at[3]),
        pltpu.make_async_copy(pot_in, pot.at[:, rows], loc_sem.at[1]),
    ]
    for c in local:
        c.start()

    bar = pltpu.get_barrier_semaphore()
    up_z, down_z = at((z + 1) % 8, y, x, core), at((z + 7) % 8, y, x, core)
    up_y, down_y = at(z, (y + 1) % 8, x, core), at(z, (y + 7) % 8, x, core)
    for to in (up_y, down_y, to_xn, to_xp, up_z, down_z, mate):
        pl.semaphore_signal(bar, inc=1, device_id=to, device_id_type=MESH)
    pl.semaphore_wait(bar, 7)
    for c in local:
        c.wait()

    far_z = (at((z + 2) % 8, y, x, core), at((z + 6) % 8, y, x, core))
    far_y = (at(z, (y + 2) % 8, x, core), at(z, (y + 6) % 8, x, core))
    words = (
        (up_z, down_z), far_z, (up_y, down_y), (up_y, down_y), far_y, (mate,), (to_xn, to_xp), (to_xn, to_xp),
    )

    def tell(k):
        for to in words[k]:
            pl.semaphore_signal(ring.at[k], inc=1, device_id=to, device_id_type=MESH)

    def hear(k):
        pl.semaphore_wait(ring.at[k], len(words[k]))

    swaps = [
        rdma(
            give.at[pl.ds(k, n)], orb.at[pl.ds(k + 6, n), rows],
            in_send.at[i], in_recv.at[i], at(z, yo, x, core),
        )
        for i, (k, n) in enumerate(((0, 6), (10, 6), (6, 4)))
    ]
    direct = [
        rdma(orb.at[pl.ds(16, 6), rows], orb.at[low, rows], in_send.at[3], in_recv.at[3], to_xn),
        rdma(orb.at[pl.ds(6, 6), rows], orb.at[high, rows], in_send.at[4], in_recv.at[4], to_xp),
    ]
    given = rdma(pot.at[:, rows], pot.at[:, rows], in_send.at[5], in_recv.at[5], at(z, yq, x, core))

    def to_mate(k, src, dst):
        c = rdma(src, dst, core_send.at[k], core_recv.at[k], mate)
        c.start()
        return c

    for c in swaps[:2] + direct + [given]:
        c.start()
    beside = [to_mate(0, orb.at[mid, rows], zo.at[:, rows])]
    tell(0)

    lane = lax.broadcasted_iota(jnp.int32, (NY, CZ), 1)
    lane_half = lax.broadcasted_iota(jnp.int32, (CY, CZ), 1)

    def over_layers(body, first_layer=0, count=CX):
        def step(k, _):
            body(k)
            return 0

        lax.fori_loop(first_layer, first_layer + count, step, 0, unroll=2)

    def over_strips(src, first_layer, count, finish):
        def strip(r, _):
            at_rows = pl.ds(pl.multiple_of(r * 8, 8), 8)
            line = [src[first_layer + j, at_rows] for j in range(count + 12)]
            for i in range(count):
                total = acc[first_layer + i, at_rows]
                for s in range(1, reach + 1):
                    total = total + (-0.5 * second_coeffs[s]) * (line[i + 6 + s] + line[i + 6 - s])
                finish(first_layer + i, at_rows, line[i + 6], total)
            return 0

        lax.fori_loop(0, NY // 8, strip, 0, unroll=2)

    def along_y(src):
        def body(k):
            acc[k] = part_y(src[k + 6])

        return body

    def along_z(src, beside_src):
        def body(k):
            acc[k] = acc[k] + part_z(src[k + 6], beside_src[k], lane)

        return body

    def along_z_half(at_rows):
        def body(k):
            hf[k, at_rows] = part_z(orb[k + 6, at_rows], zo[k, at_rows], lane_half)

        return body

    def rim(src, k, to_next, at_rows=slice(None)):
        if to_next:
            c = rdma(src.at[pl.ds(16, 6), at_rows], src.at[low, at_rows], x_send.at[k], x_recv.at[k], to_xn)
        else:
            c = rdma(src.at[pl.ds(6, 6), at_rows], src.at[high, at_rows], x_send.at[k], x_recv.at[k], to_xp)
        c.start()
        return c

    beside[0].wait_recv()
    over_layers(along_z_half(rows))
    swaps[2].start()
    hear(0)
    tell(1)
    swaps[0].wait_recv()
    rims = [rim(orb, 0, False, rows_other)]
    swaps[1].wait_recv()
    rims.append(rim(orb, 1, True, rows_other))
    swaps[2].wait_recv()
    beside.append(to_mate(1, orb.at[mid, rows_other], zo.at[:, rows_other]))
    over_layers(along_y(orb))
    hear(1)
    tell(2)
    beside[1].wait_recv()
    over_layers(along_z_half(rows_other))
    given.wait_recv()

    def inner(src, finish):
        over_strips(src, 6, 4, finish)

    def edges(finish, before, src, k):
        over_strips(before, 0, 6, finish)
        sent = [rim(src, k, False)]
        over_strips(before, 10, 6, finish)
        sent.append(rim(src, k + 1, True))
        beside.append(to_mate(k // 2 + 1, src.at[mid], zf if k == 2 else zs))
        return sent

    def last_first(k, at_rows, here, total):
        h = total + hf[k, at_rows] + (pot[k, at_rows] - filter_center) * here
        first[k + 6, at_rows] = h * (1.0 / filter_half)

    inner(orb, last_first)
    for c in direct + rims:
        c.wait_recv()
    rims += edges(last_first, orb, first, 2)

    hear(2)
    tell(3)
    over_layers(along_y(first))
    hear(3)
    tell(4)
    beside[2].wait_recv()
    over_layers(along_z(first, zf))
    hear(4)
    tell(5)

    def layer_of(group, pz):
        m = pz // 2
        return (6 + m, m, 4 + m + 4 * (m // 2), 12 + m)[group]

    def send_tiles(src, skip, got, which, pz, groups, at_home=False):
        for group in groups:
            for b in range(2):
                py = (pz + group + 4 * b) % 8
                row = pl.multiple_of(16 * b + 8 * (pz % 2), 8)
                copy = rdma(
                    src.at[skip + layer_of(group, pz), pl.ds(row, 8)], got.at[zy],
                    a2a_send.at[which], a2a_recv.at[which], at(pz, py, x, core),
                )
                if at_home:
                    pl.when(py != y)(copy.start)
                else:
                    copy.start()

    def all_tiles(got, which):
        return rdma(got.at[pl.ds(0, 63)], got.at[pl.ds(0, 63)], a2a_send.at[which], a2a_recv.at[which], mate)

    def send_inner(src, skip, got, which):
        def turn(i, _):
            send_tiles(src, skip, got, which, (z + far_first(i, 4)) % 8, (0,))
            return 0

        lax.fori_loop(0, 7, turn, 0)
        send_tiles(src, skip, got, which, z, (0,), True)

    def keep_tile(src, skip, got):
        group, b = (y + 8 - z) % 4, ((y + 8 - z) % 8) // 4
        row = pl.multiple_of(16 * b + 8 * (z % 2), 8)
        for k in range(4):
            @pl.when(group == k)
            def _():
                got[zy] = src[skip + layer_of(k, z), pl.ds(row, 8)]

    def last_filtered(k, at_rows, here, total):
        h = total + (pot[k, at_rows] - filter_center) * here
        fil[k + 6, at_rows] = h * (2.0 / filter_half) - orb[k + 6, at_rows]

    inner(first, last_filtered)
    send_inner(fil, 6, gf, 0)
    for c in rims[2:4]:
        c.wait_recv()
    rims += edges(last_filtered, first, fil, 4)

    def filtered_out(i, _):
        send_tiles(fil, 6, gf, 0, (z + far_first(i, 4)) % 8, (1, 2, 3))
        for j in (2 * i, 2 * i + 1):
            acc[j] = part_y(fil[j + 6])
        return 0

    lax.fori_loop(0, 7, filtered_out, 0)
    send_tiles(fil, 6, gf, 0, z, (1, 2, 3), True)
    keep_tile(fil, 6, gf)
    for j in (14, 15):
        acc[j] = part_y(fil[j + 6])
    hear(5)
    tell(6)

    def last_applied(k, at_rows, here, total):
        hf[k, at_rows] = total + pot[k, at_rows] * here

    beside[3].wait_recv()
    over_layers(along_z(fil, zs))
    hear(6)
    tell(7)
    inner(fil, last_applied)
    send_inner(hf, 0, gh, 1)
    for c in rims[4:]:
        c.wait_recv()
    over_strips(fil, 0, 6, last_applied)
    over_strips(fil, 10, 6, last_applied)

    def applied_out(i, _):
        send_tiles(hf, 0, gh, 1, (z + far_first(i, 4)) % 8, (1, 2, 3))
        return 0

    lax.fori_loop(0, 7, applied_out, 0)
    send_tiles(hf, 0, gh, 1, z, (1, 2, 3), True)
    keep_tile(hf, 0, gh)

    def contract(left, right):
        return lax.dot_general(left, right, (((1,), (1,)), ((), ())), preferred_element_type=jnp.float32)

    def halves(value):
        upper = value.astype(jnp.bfloat16)
        return upper, (value - upper.astype(jnp.float32)).astype(jnp.bfloat16)

    def cells(got, s):
        return jnp.concatenate([got[:, 2 * s, :], got[:, 2 * s + 1, :]], axis=1)

    hear(7)
    all_tiles(gf, 0).wait_recv()
    over = jnp.zeros((NB, NB), jnp.float32)
    for s in range(4):
        upper, lower = halves(cells(gf, s))
        g_high[s] = upper
        g_low[s] = lower
        over = over + (contract(upper, upper) + (contract(upper, lower) + contract(lower, upper)))
    part[:, :, :NB] = over.reshape(32, 2, NB)
    all_tiles(gh, 1).wait_recv()
    proj = jnp.zeros((NB, NB), jnp.float32)
    for s in range(4):
        upper, lower = halves(cells(gh, s))
        proj = proj + (contract(g_high[s], upper) + (contract(g_high[s], lower) + contract(g_low[s], upper)))
    part[:, :, NB:] = proj.reshape(32, 2, NB)

    def send_rows(pz, at_home=False):
        for k in range(8):
            py = (y + far_first(k, 4)) % 8
            if not (at_home and k == 7):
                rdma(
                    part.at[pz * 4 + py // 2], r1.at[zy], red_send.at[0], red_recv.at[0], at(pz, py, x, core)
                ).start()

    def rows_out(i, _):
        send_rows((z + far_first(i, 4)) % 8)
        return 0

    lax.fori_loop(0, 7, rows_out, 0)
    send_rows(z, True)
    r1[zy] = part[band]
    red1 = rdma(r1.at[pl.ds(0, 63)], r1.at[pl.ds(0, 63)], red_send.at[0], red_recv.at[0], mate)
    red1.wait_recv()
    back = rdma(fil.at[mid, rows_other], out_f.at[yl], back_send, back_recv, at(z, yo, x, core))
    back.start()
    keep = pltpu.make_async_copy(fil.at[mid, rows], out_f.at[yl], loc_sem.at[2])
    keep.start()

    tot[...] = jnp.sum(r1[...], axis=0)
    slot = x * 2 + core
    for i in range(4):
        for pc in (1 - core, core)[: 2 if i < 3 else 1]:
            to = at(z, y, (x + far_first(i, 2)) % 4, pc)
            rdma(tot, r2.at[slot], red_send.at[1], red_recv.at[1], to).start()
    r2[slot] = tot[...]
    red2 = rdma(r2.at[pl.ds(0, 7)], r2.at[pl.ds(0, 7)], red_send.at[1], red_recv.at[1], mate)
    red2.wait_recv()
    result = jnp.sum(r2[...], axis=0) * (1.0 / NCELL)
    out_s[...] = result[:, :NB]
    out_p[...] = result[:, NB:]

    for c in swaps + direct + [given]:
        c.wait_send()
    for c in beside:
        c.wait_send()
    for c in rims:
        c.wait_send()
    all_tiles(gf, 0).wait_send()
    all_tiles(gh, 1).wait_send()
    red1.wait_send()
    red2.wait_send()
    keep.wait()
    back.wait()


def deliver(filtered, inter, proj, out_f, out_s, out_p, sem):
    copies = [
        pltpu.make_async_copy(src, dst, sem.at[i])
        for i, (src, dst) in enumerate(((filtered, out_f), (inter, out_s), (proj, out_p)))
    ]
    for c in copies:
        c.start()
    for c in copies:
        c.wait()


def shards(orbitals, potential):
    f32 = jnp.float32
    vmem = pltpu.VMEM
    dma = pltpu.SemaphoreType.DMA
    any_ = pl.BlockSpec(memory_space=pl.ANY)
    hbm = pl.BlockSpec(memory_space=pltpu.HBM)
    full = pl.BlockSpec(memory_space=pltpu.VMEM)
    filtered, inter, proj = pl.pallas_call(
        kernel,
        out_shape=(
            jax.ShapeDtypeStruct((2, CX, CY, CZ), f32),
            jax.ShapeDtypeStruct((2, NB), f32),
            jax.ShapeDtypeStruct((2, NB), f32),
        ),
        in_specs=[hbm, hbm],
        out_specs=(hbm, full, full),
        scratch_shapes=[
            vmem((CX + 12, NY, CZ), f32),
            vmem((CX, CY, CZ), f32),
            vmem((CX, NY, CZ), f32),
            vmem((CX + 12, NY, CZ), f32),
            vmem((CX + 12, NY, CZ), f32),
            vmem((CX, NY, CZ), f32),
            vmem((CX, NY, CZ), f32),
            vmem((CX, NY, CZ), f32),
            vmem((CX, NY, CZ), f32),
            vmem((CX, NY, CZ), f32),
            vmem((NB, 8, CZ), f32),
            vmem((NB, 8, CZ), f32),
            vmem((4, NB, 2 * CZ), jnp.bfloat16),
            vmem((4, NB, 2 * CZ), jnp.bfloat16),
            vmem((32, 2, 2 * NB), f32),
            vmem((64, 2, 2 * NB), f32),
            vmem((8, 2, 2 * NB), f32),
            vmem((2, 2 * NB), f32),
            dma((4,)), dma((6,)), dma((6,)), dma((4,)), dma((4,)), dma((6,)), dma((6,)),
            dma((2,)), dma((2,)), dma, dma, dma((2,)), dma((2,)),
            pltpu.SemaphoreType.REGULAR((8,)),
        ],
        compiler_params=pltpu.CompilerParams(
            collective_id=0, has_side_effects=True, vmem_limit_bytes=32 << 20
        ),
        name="chebyshev_step",
    )(
        pltpu.with_memory_space_constraint(orbitals.reshape(2, CX, CY, CZ), pltpu.HBM),
        pltpu.with_memory_space_constraint(potential.reshape(CX, CY, CZ), pltpu.HBM),
    )
    filtered, inter, proj = pl.pallas_call(
        deliver,
        out_shape=(
            jax.ShapeDtypeStruct((2, CX, CY, CZ), f32),
            jax.ShapeDtypeStruct((2, NB), f32),
            jax.ShapeDtypeStruct((2, NB), f32),
        ),
        in_specs=[any_, any_, any_],
        out_specs=(hbm, hbm, hbm),
        scratch_shapes=[dma((3,))],
        compiler_params=pltpu.CompilerParams(vmem_limit_bytes=32 << 20),
        name="deliver",
    )(filtered, inter, proj)
    return filtered[:, None], inter, proj


def solution(mesh):
    return jax.shard_map(
        shards,
        mesh=mesh,
        in_specs=(P("band", "domain", None, None, None), P("domain", None, None, None)),
        out_specs=(P("band", "domain", None, None, None), P("band", None), P("band", None)),
        check_vma=False,
    )
```

```python
import functools

import jax
import jax.numpy as jnp
from jax import lax
from jax.experimental import pallas as pl
from jax.experimental.pallas import tpu as pltpu
from jax.sharding import PartitionSpec as P

second_coeffs = (
    -5369.0 / 1800.0,
    12.0 / 7.0,
    -15.0 / 56.0,
    10.0 / 189.0,
    -1.0 / 112.0,
    2.0 / 1925.0,
    -1.0 / 16632.0,
)
filter_center = 6.5
filter_half = 5.5
reach = 6
MESH = pl.DeviceIdType.MESH

CX, CY, CZ = 16, 16, 128
NY = 32
NB = 64
NCELL = 524288


def part_y(here):
    total = (-1.5 * second_coeffs[0]) * here
    for s in range(1, reach + 1):
        pair = pltpu.roll(here, s, 0) + pltpu.roll(here, NY - s, 0)
        total = total + (-0.5 * second_coeffs[s]) * pair
    return total


def part_z(here, beside, lane):
    total = None
    for s in range(1, reach + 1):
        ahead = pltpu.roll(jnp.where(lane < s, beside, here), CZ - s, 1)
        behind = pltpu.roll(jnp.where(lane >= CZ - s, beside, here), s, 1)
        term = (-0.5 * second_coeffs[s]) * (ahead + behind)
        total = term if total is None else total + term
    return total


def far_first(i, half):
    return half + ((i + 1) // 2) * (2 * (i % 2) - 1)


def kernel(
    orb_in, pot_in, out_f, out_s, out_p,
    orb, give, pot, first, fil, zo, zf, zs, acc, hf, gf, gh, g_high, g_low, part, r1, r2, tot,
    loc_sem, in_send, in_recv, core_send, core_recv, x_send, x_recv,
    a2a_send, a2a_recv, back_send, back_recv, red_send, red_recv, ring,
):
    band = lax.axis_index("band")
    domain = lax.axis_index("domain")
    z, yh = band // 4, band % 4
    x, yl, core = domain // 4, (domain // 2) % 2, domain % 2
    y = yh * 2 + yl
    zy = z * 8 + y
    mine = pl.multiple_of(yl * CY, CY)
    other = pl.multiple_of((1 - yl) * CY, CY)

    def at(pz, py, px, pc):
        return (pz * 4 + py // 2, px * 4 + (py % 2) * 2 + pc)

    xn, xp = (x + 1) % 4, (x + 3) % 4
    yo = y + 1 - 2 * yl
    yq = (y + 7 + 2 * yl) % 8
    mate = at(z, y, x, 1 - core)
    to_xn, to_xp = at(z, y, xn, core), at(z, y, xp, core)

    def rdma(src, dst, send, recv, to):
        return pltpu.make_async_remote_copy(
            src_ref=src, dst_ref=dst, send_sem=send, recv_sem=recv,
            device_id=to, device_id_type=MESH,
        )

    mid = pl.ds(6, CX)
    low, high = pl.ds(0, 6), pl.ds(22, 6)
    rows = pl.ds(mine, CY)
    rows_other = pl.ds(other, CY)

    local = [
        pltpu.make_async_copy(orb_in.at[yl], orb.at[mid, rows], loc_sem.at[0]),
        pltpu.make_async_copy(orb_in.at[1 - yl], give, loc_sem.at[3]),
        pltpu.make_async_copy(pot_in, pot.at[:, rows], loc_sem.at[1]),
    ]
    for c in local:
        c.start()

    bar = pltpu.get_barrier_semaphore()
    up_z, down_z = at((z + 1) % 8, y, x, core), at((z + 7) % 8, y, x, core)
    up_y, down_y = at(z, (y + 1) % 8, x, core), at(z, (y + 7) % 8, x, core)
    for to in (up_y, down_y, to_xn, to_xp, up_z, down_z, mate):
        pl.semaphore_signal(bar, inc=1, device_id=to, device_id_type=MESH)
    pl.semaphore_wait(bar, 7)
    for c in local:
        c.wait()

    far_z = (at((z + 2) % 8, y, x, core), at((z + 6) % 8, y, x, core))
    far_y = (at(z, (y + 2) % 8, x, core), at(z, (y + 6) % 8, x, core))
    words = (
        (up_z, down_z), far_z, (up_y, down_y), (up_y, down_y), far_y, (mate,), (to_xn, to_xp), (to_xn, to_xp),
    )

    def tell(k):
        for to in words[k]:
            pl.semaphore_signal(ring.at[k], inc=1, device_id=to, device_id_type=MESH)

    def hear(k):
        pl.semaphore_wait(ring.at[k], len(words[k]))

    swaps = [
        rdma(
            give.at[pl.ds(k, n)], orb.at[pl.ds(k + 6, n), rows],
            in_send.at[i], in_recv.at[i], at(z, yo, x, core),
        )
        for i, (k, n) in enumerate(((0, 6), (10, 6), (6, 4)))
    ]
    direct = [
        rdma(orb.at[pl.ds(16, 6), rows], orb.at[low, rows], in_send.at[3], in_recv.at[3], to_xn),
        rdma(orb.at[pl.ds(6, 6), rows], orb.at[high, rows], in_send.at[4], in_recv.at[4], to_xp),
    ]
    given = rdma(pot.at[:, rows], pot.at[:, rows], in_send.at[5], in_recv.at[5], at(z, yq, x, core))

    def to_mate(k, src, dst):
        c = rdma(src, dst, core_send.at[k], core_recv.at[k], mate)
        c.start()
        return c

    for c in swaps[:2] + direct + [given]:
        c.start()
    beside = [to_mate(0, orb.at[mid, rows], zo.at[:, rows])]
    tell(0)

    lane = lax.broadcasted_iota(jnp.int32, (NY, CZ), 1)
    lane_half = lax.broadcasted_iota(jnp.int32, (CY, CZ), 1)

    def over_layers(body, first_layer=0, count=CX):
        def step(k, _):
            body(k)
            return 0

        lax.fori_loop(first_layer, first_layer + count, step, 0, unroll=2)

    def over_strips(src, first_layer, count, finish, base=0, strips=NY // 8):
        def strip(r, _):
            at_rows = pl.ds(pl.multiple_of(base + r * 8, 8), 8)
            line = [src[first_layer + j, at_rows] for j in range(count + 12)]
            for i in range(count):
                total = acc[first_layer + i, at_rows]
                for s in range(1, reach + 1):
                    total = total + (-0.5 * second_coeffs[s]) * (line[i + 6 + s] + line[i + 6 - s])
                finish(first_layer + i, at_rows, line[i + 6], total)
            return 0

        lax.fori_loop(0, strips, strip, 0, unroll=2)

    def along_y(src):
        def body(k):
            acc[k] = part_y(src[k + 6])

        return body

    def along_z(src, beside_src):
        def body(k):
            acc[k] = acc[k] + part_z(src[k + 6], beside_src[k], lane)

        return body

    def along_z_half(at_rows):
        def body(k):
            hf[k, at_rows] = part_z(orb[k + 6, at_rows], zo[k, at_rows], lane_half)

        return body

    def rim(src, k, to_next, at_rows=slice(None)):
        if to_next:
            c = rdma(src.at[pl.ds(16, 6), at_rows], src.at[low, at_rows], x_send.at[k], x_recv.at[k], to_xn)
        else:
            c = rdma(src.at[pl.ds(6, 6), at_rows], src.at[high, at_rows], x_send.at[k], x_recv.at[k], to_xp)
        c.start()
        return c

    beside[0].wait_recv()
    over_layers(along_z_half(rows))
    swaps[2].start()
    hear(0)
    tell(1)
    swaps[0].wait_recv()
    rims = [rim(orb, 0, False, rows_other)]
    swaps[1].wait_recv()
    rims.append(rim(orb, 1, True, rows_other))
    swaps[2].wait_recv()
    beside.append(to_mate(1, orb.at[mid, rows_other], zo.at[:, rows_other]))
    over_layers(along_y(orb))
    hear(1)
    tell(2)
    beside[1].wait_recv()
    over_layers(along_z_half(rows_other))
    given.wait_recv()

    def inner(src, finish):
        over_strips(src, 6, 4, finish)

    def edges(finish, before, arriving, src, k):
        sent = []
        for h, (base, at_rows) in enumerate(((mine, rows), (other, rows_other))):
            for c in arriving[h]:
                c.wait_recv()
            over_strips(before, 0, 6, finish, base, 2)
            sent.append([rim(src, k + 2 * h, False, at_rows)])
            over_strips(before, 10, 6, finish, base, 2)
            sent[h].append(rim(src, k + 2 * h + 1, True, at_rows))
        beside.append(to_mate(k // 4 + 2, src.at[mid], zf if k == 2 else zs))
        return sent

    def last_first(k, at_rows, here, total):
        h = total + hf[k, at_rows] + (pot[k, at_rows] - filter_center) * here
        first[k + 6, at_rows] = h * (1.0 / filter_half)

    inner(orb, last_first)
    rims_first = edges(last_first, orb, (direct, rims), first, 2)

    hear(2)
    tell(3)
    over_layers(along_y(first))
    hear(3)
    tell(4)
    beside[2].wait_recv()
    over_layers(along_z(first, zf))
    hear(4)
    tell(5)

    def layer_of(group, pz):
        m = pz // 2
        return (6 + m, m, 4 + m + 4 * (m // 2), 12 + m)[group]

    def send_tiles(src, skip, got, which, pz, groups, at_home=False, parts=(0, 1)):
        for group in groups:
            for b in parts:
                py = (pz + group + 4 * b) % 8
                row = pl.multiple_of(16 * b + 8 * (pz % 2), 8)
                copy = rdma(
                    src.at[skip + layer_of(group, pz), pl.ds(row, 8)], got.at[zy],
                    a2a_send.at[which], a2a_recv.at[which], at(pz, py, x, core),
                )
                if at_home:
                    pl.when(py != y)(copy.start)
                else:
                    copy.start()

    def all_tiles(got, which):
        return rdma(got.at[pl.ds(0, 63)], got.at[pl.ds(0, 63)], a2a_send.at[which], a2a_recv.at[which], mate)

    def send_all(src, skip, got, which, groups, parts=(0, 1), work=None):
        def turn(i, _):
            send_tiles(src, skip, got, which, (z + far_first(i, 4)) % 8, groups, False, parts)
            if work is not None:
                work(2 * i)
                work(2 * i + 1)
            return 0

        lax.fori_loop(0, 7, turn, 0)
        send_tiles(src, skip, got, which, z, groups, True, parts)
        if work is not None:
            work(14)
            work(15)

    def keep_tile(src, skip, got):
        group, b = (y + 8 - z) % 4, ((y + 8 - z) % 8) // 4
        row = pl.multiple_of(16 * b + 8 * (z % 2), 8)
        for k in range(4):
            @pl.when(group == k)
            def _():
                got[zy] = src[skip + layer_of(k, z), pl.ds(row, 8)]

    def last_filtered(k, at_rows, here, total):
        h = total + (pot[k, at_rows] - filter_center) * here
        fil[k + 6, at_rows] = h * (2.0 / filter_half) - orb[k + 6, at_rows]

    inner(first, last_filtered)
    rims_filtered = edges(last_filtered, first, rims_first, fil, 6)

    send_all(fil, 6, gf, 0, (0, 1), work=along_y(fil))
    keep_tile(fil, 6, gf)
    hear(5)
    tell(6)

    def last_applied(k, at_rows, here, total):
        hf[k, at_rows] = total + pot[k, at_rows] * here

    beside[3].wait_recv()
    send_all(fil, 6, gf, 0, (2, 3), work=along_z(fil, zs))
    hear(6)
    tell(7)
    inner(fil, last_applied)
    send_all(hf, 0, gh, 1, (0,))
    for h, base in enumerate((mine, other)):
        for c in rims_filtered[h]:
            c.wait_recv()
        over_strips(fil, 0, 6, last_applied, base, 2)
        over_strips(fil, 10, 6, last_applied, base, 2)
        send_all(hf, 0, gh, 1, (1, 2, 3), (yl if h == 0 else 1 - yl,))
    keep_tile(hf, 0, gh)

    def contract(left, right):
        return lax.dot_general(left, right, (((1,), (1,)), ((), ())), preferred_element_type=jnp.float32)

    def halves(value):
        upper = value.astype(jnp.bfloat16)
        return upper, (value - upper.astype(jnp.float32)).astype(jnp.bfloat16)

    def cells(got, s):
        return jnp.concatenate([got[:, 2 * s, :], got[:, 2 * s + 1, :]], axis=1)

    hear(7)
    all_tiles(gf, 0).wait_recv()
    over = jnp.zeros((NB, NB), jnp.float32)
    for s in range(4):
        upper, lower = halves(cells(gf, s))
        g_high[s] = upper
        g_low[s] = lower
        over = over + (contract(upper, upper) + (contract(upper, lower) + contract(lower, upper)))
    part[:, :, :NB] = over.reshape(32, 2, NB)
    all_tiles(gh, 1).wait_recv()
    proj = jnp.zeros((NB, NB), jnp.float32)
    for s in range(4):
        upper, lower = halves(cells(gh, s))
        proj = proj + (contract(g_high[s], upper) + (contract(g_high[s], lower) + contract(g_low[s], upper)))
    part[:, :, NB:] = proj.reshape(32, 2, NB)

    def send_rows(pz, at_home=False):
        for k in range(8):
            py = (y + far_first(k, 4)) % 8
            if not (at_home and k == 7):
                rdma(
                    part.at[pz * 4 + py // 2], r1.at[zy], red_send.at[0], red_recv.at[0], at(pz, py, x, core)
                ).start()

    def rows_out(i, _):
        send_rows((z + far_first(i, 4)) % 8)
        return 0

    lax.fori_loop(0, 7, rows_out, 0)
    send_rows(z, True)
    back = rdma(fil.at[mid, rows_other], out_f.at[yl], back_send, back_recv, at(z, yo, x, core))
    back.start()
    keep = pltpu.make_async_copy(fil.at[mid, rows], out_f.at[yl], loc_sem.at[2])
    keep.start()
    r1[zy] = part[band]
    red1 = rdma(r1.at[pl.ds(0, 63)], r1.at[pl.ds(0, 63)], red_send.at[0], red_recv.at[0], mate)
    red1.wait_recv()
    tot[...] = jnp.sum(r1[...], axis=0)
    slot = x * 2 + core
    for i in range(4):
        for pc in (1 - core, core)[: 2 if i < 3 else 1]:
            to = at(z, y, (x + far_first(i, 2)) % 4, pc)
            rdma(tot, r2.at[slot], red_send.at[1], red_recv.at[1], to).start()
    r2[slot] = tot[...]
    red2 = rdma(r2.at[pl.ds(0, 7)], r2.at[pl.ds(0, 7)], red_send.at[1], red_recv.at[1], mate)
    red2.wait_recv()
    result = jnp.sum(r2[...], axis=0) * (1.0 / NCELL)
    out_s[...] = result[:, :NB]
    out_p[...] = result[:, NB:]

    for c in swaps + direct + [given] + rims:
        c.wait_send()
    for c in beside:
        c.wait_send()
    for c in sum(rims_first, []):
        c.wait_send()
    for c in sum(rims_filtered, []):
        c.wait_send()
    all_tiles(gf, 0).wait_send()
    all_tiles(gh, 1).wait_send()
    red1.wait_send()
    red2.wait_send()
    keep.wait()
    back.wait()


def deliver(filtered, inter, proj, out_f, out_s, out_p, sem):
    copies = [
        pltpu.make_async_copy(src, dst, sem.at[i])
        for i, (src, dst) in enumerate(((filtered, out_f), (inter, out_s), (proj, out_p)))
    ]
    for c in copies:
        c.start()
    for c in copies:
        c.wait()


def shards(orbitals, potential):
    f32 = jnp.float32
    vmem = pltpu.VMEM
    dma = pltpu.SemaphoreType.DMA
    any_ = pl.BlockSpec(memory_space=pl.ANY)
    hbm = pl.BlockSpec(memory_space=pltpu.HBM)
    full = pl.BlockSpec(memory_space=pltpu.VMEM)
    filtered, inter, proj = pl.pallas_call(
        kernel,
        out_shape=(
            jax.ShapeDtypeStruct((2, CX, CY, CZ), f32),
            jax.ShapeDtypeStruct((2, NB), f32),
            jax.ShapeDtypeStruct((2, NB), f32),
        ),
        in_specs=[hbm, hbm],
        out_specs=(hbm, full, full),
        scratch_shapes=[
            vmem((CX + 12, NY, CZ), f32),
            vmem((CX, CY, CZ), f32),
            vmem((CX, NY, CZ), f32),
            vmem((CX + 12, NY, CZ), f32),
            vmem((CX + 12, NY, CZ), f32),
            vmem((CX, NY, CZ), f32),
            vmem((CX, NY, CZ), f32),
            vmem((CX, NY, CZ), f32),
            vmem((CX, NY, CZ), f32),
            vmem((CX, NY, CZ), f32),
            vmem((NB, 8, CZ), f32),
            vmem((NB, 8, CZ), f32),
            vmem((4, NB, 2 * CZ), jnp.bfloat16),
            vmem((4, NB, 2 * CZ), jnp.bfloat16),
            vmem((32, 2, 2 * NB), f32),
            vmem((64, 2, 2 * NB), f32),
            vmem((8, 2, 2 * NB), f32),
            vmem((2, 2 * NB), f32),
            dma((4,)), dma((6,)), dma((6,)), dma((4,)), dma((4,)), dma((10,)), dma((10,)),
            dma((2,)), dma((2,)), dma, dma, dma((2,)), dma((2,)),
            pltpu.SemaphoreType.REGULAR((8,)),
        ],
        compiler_params=pltpu.CompilerParams(
            collective_id=0, has_side_effects=True, vmem_limit_bytes=32 << 20
        ),
        name="chebyshev_step",
    )(
        pltpu.with_memory_space_constraint(orbitals.reshape(2, CX, CY, CZ), pltpu.HBM),
        pltpu.with_memory_space_constraint(potential.reshape(CX, CY, CZ), pltpu.HBM),
    )
    filtered, inter, proj = pl.pallas_call(
        deliver,
        out_shape=(
            jax.ShapeDtypeStruct((2, CX, CY, CZ), f32),
            jax.ShapeDtypeStruct((2, NB), f32),
            jax.ShapeDtypeStruct((2, NB), f32),
        ),
        in_specs=[any_, any_, any_],
        out_specs=(hbm, hbm, hbm),
        scratch_shapes=[dma((3,))],
        compiler_params=pltpu.CompilerParams(vmem_limit_bytes=32 << 20),
        name="deliver",
    )(filtered, inter, proj)
    return filtered[:, None], inter, proj


def solution(mesh):
    return jax.shard_map(
        shards,
        mesh=mesh,
        in_specs=(P("band", "domain", None, None, None), P("domain", None, None, None)),
        out_specs=(P("band", "domain", None, None, None), P("band", None), P("band", None)),
        check_vma=False,
    )
```

```python
import functools

import jax
import jax.numpy as jnp
from jax import lax
from jax.experimental import pallas as pl
from jax.experimental.pallas import tpu as pltpu
from jax.sharding import PartitionSpec as P

second_coeffs = (
    -5369.0 / 1800.0,
    12.0 / 7.0,
    -15.0 / 56.0,
    10.0 / 189.0,
    -1.0 / 112.0,
    2.0 / 1925.0,
    -1.0 / 16632.0,
)
filter_center = 6.5
filter_half = 5.5
reach = 6
MESH = pl.DeviceIdType.MESH

CX, CY, CZ = 16, 16, 128
NY = 32
NB = 64
NCELL = 524288


def part_y(here):
    total = (-1.5 * second_coeffs[0]) * here
    for s in range(1, reach + 1):
        pair = pltpu.roll(here, s, 0) + pltpu.roll(here, NY - s, 0)
        total = total + (-0.5 * second_coeffs[s]) * pair
    return total


def part_z(here, beside, lane):
    total = None
    for s in range(1, reach + 1):
        ahead = pltpu.roll(jnp.where(lane < s, beside, here), CZ - s, 1)
        behind = pltpu.roll(jnp.where(lane >= CZ - s, beside, here), s, 1)
        term = (-0.5 * second_coeffs[s]) * (ahead + behind)
        total = term if total is None else total + term
    return total


def far_first(i, half):
    return half + ((i + 1) >> 1) * (2 * (i & 1) - 1)


def kernel(
    orb_in, pot_in, out_f, out_s, out_p,
    orb, give, pot, first, fil, zo, zf, zs, acc, hf, gf, gh, g_high, g_low, part, r1, r2, tot,
    loc_sem, in_send, in_recv, core_send, core_recv, x_send, x_recv,
    a2a_send, a2a_recv, back_send, back_recv, red_send, red_recv, ring,
):
    band = lax.axis_index("band")
    domain = lax.axis_index("domain")
    z, yh = band >> 2, band & 3
    x, yl, core = domain >> 2, (domain >> 1) & 1, domain & 1
    y = yh * 2 + yl
    zy = z * 8 + y
    mine = pl.multiple_of(yl * CY, CY)
    other = pl.multiple_of((1 - yl) * CY, CY)

    def at(pz, py, px, pc):
        return ((pz << 2) + (py >> 1), (px << 2) + ((py & 1) << 1) + pc)

    xn, xp = (x + 1) & 3, (x + 3) & 3
    yo = y + 1 - 2 * yl
    yq = (y + 7 + 2 * yl) & 7
    mate = at(z, y, x, 1 - core)
    to_xn, to_xp = at(z, y, xn, core), at(z, y, xp, core)

    def rdma(src, dst, send, recv, to):
        return pltpu.make_async_remote_copy(
            src_ref=src, dst_ref=dst, send_sem=send, recv_sem=recv,
            device_id=to, device_id_type=MESH,
        )

    mid = pl.ds(6, CX)
    low, high = pl.ds(0, 6), pl.ds(22, 6)
    rows = pl.ds(mine, CY)
    rows_other = pl.ds(other, CY)

    local = [
        pltpu.make_async_copy(orb_in.at[yl], orb.at[mid, rows], loc_sem.at[0]),
        pltpu.make_async_copy(orb_in.at[1 - yl], give, loc_sem.at[3]),
        pltpu.make_async_copy(pot_in, pot.at[:, rows], loc_sem.at[1]),
    ]
    for c in local:
        c.start()

    bar = pltpu.get_barrier_semaphore()
    up_z, down_z = at((z + 1) & 7, y, x, core), at((z + 7) & 7, y, x, core)
    up_y, down_y = at(z, (y + 1) & 7, x, core), at(z, (y + 7) & 7, x, core)
    for to in (up_y, down_y, to_xn, to_xp, up_z, down_z, mate):
        pl.semaphore_signal(bar, inc=1, device_id=to, device_id_type=MESH)
    pl.semaphore_wait(bar, 7)
    for c in local:
        c.wait()

    far_z = (at((z + 2) & 7, y, x, core), at((z + 6) & 7, y, x, core))
    far_y = (at(z, (y + 2) & 7, x, core), at(z, (y + 6) & 7, x, core))
    words = (
        (up_z, down_z), far_z, (up_y, down_y), (up_y, down_y), far_y, (mate,), (to_xn, to_xp), (to_xn, to_xp),
    )

    def tell(k):
        for to in words[k]:
            pl.semaphore_signal(ring.at[k], inc=1, device_id=to, device_id_type=MESH)

    def hear(k):
        pl.semaphore_wait(ring.at[k], len(words[k]))

    swaps = [
        rdma(
            give.at[pl.ds(k, n)], orb.at[pl.ds(k + 6, n), rows],
            in_send.at[i], in_recv.at[i], at(z, yo, x, core),
        )
        for i, (k, n) in enumerate(((0, 6), (10, 6), (6, 4)))
    ]
    direct = [
        rdma(orb.at[pl.ds(16, 6), rows], orb.at[low, rows], in_send.at[3], in_recv.at[3], to_xn),
        rdma(orb.at[pl.ds(6, 6), rows], orb.at[high, rows], in_send.at[4], in_recv.at[4], to_xp),
    ]
    given = rdma(pot.at[:, rows], pot.at[:, rows], in_send.at[5], in_recv.at[5], at(z, yq, x, core))

    def to_mate(k, src, dst):
        c = rdma(src, dst, core_send.at[k], core_recv.at[k], mate)
        c.start()
        return c

    for c in swaps[:2] + direct + [given]:
        c.start()
    beside = [to_mate(0, orb.at[mid, rows], zo.at[:, rows])]
    tell(0)

    lane = lax.broadcasted_iota(jnp.int32, (NY, CZ), 1)
    lane_half = lax.broadcasted_iota(jnp.int32, (CY, CZ), 1)

    def over_layers(body, first_layer=0, count=CX):
        def step(k, _):
            body(k)
            return 0

        lax.fori_loop(first_layer, first_layer + count, step, 0, unroll=2)

    def over_strips(src, first_layer, count, finish, base=0, strips=NY // 8):
        def strip(r, _):
            at_rows = pl.ds(pl.multiple_of(base + r * 8, 8), 8)
            line = [src[first_layer + j, at_rows] for j in range(count + 12)]
            for i in range(count):
                total = acc[first_layer + i, at_rows]
                for s in range(1, reach + 1):
                    total = total + (-0.5 * second_coeffs[s]) * (line[i + 6 + s] + line[i + 6 - s])
                finish(first_layer + i, at_rows, line[i + 6], total)
            return 0

        lax.fori_loop(0, strips, strip, 0, unroll=2)

    def along_y(src):
        def body(k):
            acc[k] = part_y(src[k + 6])

        return body

    def along_z(src, beside_src):
        def body(k):
            acc[k] = acc[k] + part_z(src[k + 6], beside_src[k], lane)

        return body

    def along_z_half(at_rows):
        def body(k):
            hf[k, at_rows] = part_z(orb[k + 6, at_rows], zo[k, at_rows], lane_half)

        return body

    def rim(src, k, to_next, at_rows=slice(None)):
        if to_next:
            c = rdma(src.at[pl.ds(16, 6), at_rows], src.at[low, at_rows], x_send.at[k], x_recv.at[k], to_xn)
        else:
            c = rdma(src.at[pl.ds(6, 6), at_rows], src.at[high, at_rows], x_send.at[k], x_recv.at[k], to_xp)
        c.start()
        return c

    beside[0].wait_recv()
    over_layers(along_z_half(rows))
    swaps[2].start()
    hear(0)
    tell(1)
    swaps[0].wait_recv()
    rims = [rim(orb, 0, False, rows_other)]
    swaps[1].wait_recv()
    rims.append(rim(orb, 1, True, rows_other))
    swaps[2].wait_recv()
    beside.append(to_mate(1, orb.at[mid, rows_other], zo.at[:, rows_other]))
    over_layers(along_y(orb))
    hear(1)
    tell(2)
    beside[1].wait_recv()
    over_layers(along_z_half(rows_other))
    given.wait_recv()

    def inner(src, finish):
        over_strips(src, 6, 4, finish)

    def edges(finish, before, arriving, src, k):
        sent = []
        for h, (base, at_rows) in enumerate(((mine, rows), (other, rows_other))):
            for c in arriving[h]:
                c.wait_recv()
            over_strips(before, 0, 6, finish, base, 2)
            sent.append([rim(src, k + 2 * h, False, at_rows)])
            over_strips(before, 10, 6, finish, base, 2)
            sent[h].append(rim(src, k + 2 * h + 1, True, at_rows))
        beside.append(to_mate(k // 4 + 2, src.at[mid], zf if k == 2 else zs))
        return sent

    def last_first(k, at_rows, here, total):
        h = total + hf[k, at_rows] + (pot[k, at_rows] - filter_center) * here
        first[k + 6, at_rows] = h * (1.0 / filter_half)

    inner(orb, last_first)
    rims_first = edges(last_first, orb, (direct, rims), first, 2)

    hear(2)
    tell(3)
    over_layers(along_y(first))
    hear(3)
    tell(4)
    beside[2].wait_recv()
    over_layers(along_z(first, zf))
    hear(4)
    tell(5)

    def layer_of(group, pz):
        m = pz >> 1
        return (6 + m, m, 4 + m + ((m >> 1) << 2), 12 + m)[group]

    def send_tiles(src, skip, got, which, pz, groups, at_home=False, parts=(0, 1)):
        for group in groups:
            for b in parts:
                py = (pz + group + 4 * b) & 7
                row = pl.multiple_of(16 * b + ((pz & 1) << 3), 8)
                copy = rdma(
                    src.at[skip + layer_of(group, pz), pl.ds(row, 8)], got.at[zy],
                    a2a_send.at[which], a2a_recv.at[which], at(pz, py, x, core),
                )
                if at_home:
                    pl.when(py != y)(copy.start)
                else:
                    copy.start()

    def all_tiles(got, which):
        return rdma(got.at[pl.ds(0, 63)], got.at[pl.ds(0, 63)], a2a_send.at[which], a2a_recv.at[which], mate)

    def send_all(src, skip, got, which, groups, parts=(0, 1), work=None):
        def turn(i, _):
            send_tiles(src, skip, got, which, (z + far_first(i, 4)) & 7, groups, False, parts)
            if work is not None:
                work(2 * i)
                work(2 * i + 1)
            return 0

        lax.fori_loop(0, 7, turn, 0)
        send_tiles(src, skip, got, which, z, groups, True, parts)
        if work is not None:
            work(14)
            work(15)

    def keep_tile(src, skip, got):
        group, b = (y + 8 - z) & 3, ((y + 8 - z) & 7) >> 2
        row = pl.multiple_of(16 * b + ((z & 1) << 3), 8)
        for k in range(4):
            @pl.when(group == k)
            def _():
                got[zy] = src[skip + layer_of(k, z), pl.ds(row, 8)]

    def last_filtered(k, at_rows, here, total):
        h = total + (pot[k, at_rows] - filter_center) * here
        fil[k + 6, at_rows] = h * (2.0 / filter_half) - orb[k + 6, at_rows]

    inner(first, last_filtered)
    send_all(fil, 6, gf, 0, (0,))
    rims_filtered = edges(last_filtered, first, rims_first, fil, 6)

    send_all(fil, 6, gf, 0, (1, 2, 3), work=along_y(fil))
    keep_tile(fil, 6, gf)
    hear(5)
    tell(6)

    def last_applied(k, at_rows, here, total):
        hf[k, at_rows] = total + pot[k, at_rows] * here

    beside[3].wait_recv()
    over_layers(along_z(fil, zs))
    hear(6)
    tell(7)
    inner(fil, last_applied)
    send_all(hf, 0, gh, 1, (0,))
    for h, base in enumerate((mine, other)):
        for c in rims_filtered[h]:
            c.wait_recv()
        over_strips(fil, 0, 6, last_applied, base, 2)
        over_strips(fil, 10, 6, last_applied, base, 2)
    send_all(hf, 0, gh, 1, (1, 2, 3))
    keep_tile(hf, 0, gh)

    def contract(left, right):
        return lax.dot_general(left, right, (((1,), (1,)), ((), ())), preferred_element_type=jnp.float32)

    def halves(value):
        upper = value.astype(jnp.bfloat16)
        return upper, (value - upper.astype(jnp.float32)).astype(jnp.bfloat16)

    def cells(got, s):
        return jnp.concatenate([got[:, 2 * s, :], got[:, 2 * s + 1, :]], axis=1)

    hear(7)
    all_tiles(gf, 0).wait_recv()
    over = jnp.zeros((NB, NB), jnp.float32)
    for s in range(4):
        upper, lower = halves(cells(gf, s))
        g_high[s] = upper
        g_low[s] = lower
        over = over + (contract(upper, upper) + (contract(upper, lower) + contract(lower, upper)))
    part[:, :, :NB] = over.reshape(32, 2, NB)
    all_tiles(gh, 1).wait_recv()
    proj = jnp.zeros((NB, NB), jnp.float32)
    for s in range(4):
        upper, lower = halves(cells(gh, s))
        proj = proj + (contract(g_high[s], upper) + (contract(g_high[s], lower) + contract(g_low[s], upper)))
    part[:, :, NB:] = proj.reshape(32, 2, NB)

    def send_rows(pz, at_home=False):
        for k in range(8):
            py = (y + far_first(k, 4)) & 7
            if not (at_home and k == 7):
                rdma(
                    part.at[(pz << 2) + (py >> 1)], r1.at[zy], red_send.at[0], red_recv.at[0], at(pz, py, x, core)
                ).start()

    def rows_out(i, _):
        send_rows((z + far_first(i, 4)) & 7)
        return 0

    lax.fori_loop(0, 7, rows_out, 0)
    send_rows(z, True)
    back = rdma(fil.at[mid, rows_other], out_f.at[yl], back_send, back_recv, at(z, yo, x, core))
    back.start()
    keep = pltpu.make_async_copy(fil.at[mid, rows], out_f.at[yl], loc_sem.at[2])
    keep.start()
    r1[zy] = part[band]
    red1 = rdma(r1.at[pl.ds(0, 63)], r1.at[pl.ds(0, 63)], red_send.at[0], red_recv.at[0], mate)
    red1.wait_recv()
    tot[...] = jnp.sum(r1[...], axis=0)
    slot = x * 2 + core
    for i in range(4):
        for pc in (1 - core, core)[: 2 if i < 3 else 1]:
            to = at(z, y, (x + far_first(i, 2)) & 3, pc)
            rdma(tot, r2.at[slot], red_send.at[1], red_recv.at[1], to).start()
    r2[slot] = tot[...]
    red2 = rdma(r2.at[pl.ds(0, 7)], r2.at[pl.ds(0, 7)], red_send.at[1], red_recv.at[1], mate)
    red2.wait_recv()
    result = jnp.sum(r2[...], axis=0) * (1.0 / NCELL)
    out_s[...] = result[:, :NB]
    out_p[...] = result[:, NB:]

    for c in swaps + direct + [given] + rims:
        c.wait_send()
    for c in beside:
        c.wait_send()
    for c in sum(rims_first, []):
        c.wait_send()
    for c in sum(rims_filtered, []):
        c.wait_send()
    all_tiles(gf, 0).wait_send()
    all_tiles(gh, 1).wait_send()
    red1.wait_send()
    red2.wait_send()
    keep.wait()
    back.wait()


def deliver(filtered, inter, proj, out_f, out_s, out_p, sem):
    copies = [
        pltpu.make_async_copy(src, dst, sem.at[i])
        for i, (src, dst) in enumerate(((filtered, out_f), (inter, out_s), (proj, out_p)))
    ]
    for c in copies:
        c.start()
    for c in copies:
        c.wait()


def shards(orbitals, potential):
    f32 = jnp.float32
    vmem = pltpu.VMEM
    dma = pltpu.SemaphoreType.DMA
    any_ = pl.BlockSpec(memory_space=pl.ANY)
    hbm = pl.BlockSpec(memory_space=pltpu.HBM)
    full = pl.BlockSpec(memory_space=pltpu.VMEM)
    filtered, inter, proj = pl.pallas_call(
        kernel,
        out_shape=(
            jax.ShapeDtypeStruct((2, CX, CY, CZ), f32),
            jax.ShapeDtypeStruct((2, NB), f32),
            jax.ShapeDtypeStruct((2, NB), f32),
        ),
        in_specs=[hbm, hbm],
        out_specs=(hbm, full, full),
        scratch_shapes=[
            vmem((CX + 12, NY, CZ), f32),
            vmem((CX, CY, CZ), f32),
            vmem((CX, NY, CZ), f32),
            vmem((CX + 12, NY, CZ), f32),
            vmem((CX + 12, NY, CZ), f32),
            vmem((CX, NY, CZ), f32),
            vmem((CX, NY, CZ), f32),
            vmem((CX, NY, CZ), f32),
            vmem((CX, NY, CZ), f32),
            vmem((CX, NY, CZ), f32),
            vmem((NB, 8, CZ), f32),
            vmem((NB, 8, CZ), f32),
            vmem((4, NB, 2 * CZ), jnp.bfloat16),
            vmem((4, NB, 2 * CZ), jnp.bfloat16),
            vmem((32, 2, 2 * NB), f32),
            vmem((64, 2, 2 * NB), f32),
            vmem((8, 2, 2 * NB), f32),
            vmem((2, 2 * NB), f32),
            dma((4,)), dma((6,)), dma((6,)), dma((4,)), dma((4,)), dma((10,)), dma((10,)),
            dma((2,)), dma((2,)), dma, dma, dma((2,)), dma((2,)),
            pltpu.SemaphoreType.REGULAR((8,)),
        ],
        compiler_params=pltpu.CompilerParams(
            collective_id=0, has_side_effects=True, vmem_limit_bytes=32 << 20
        ),
        name="chebyshev_step",
    )(
        pltpu.with_memory_space_constraint(orbitals.reshape(2, CX, CY, CZ), pltpu.HBM),
        pltpu.with_memory_space_constraint(potential.reshape(CX, CY, CZ), pltpu.HBM),
    )
    filtered, inter, proj = pl.pallas_call(
        deliver,
        out_shape=(
            jax.ShapeDtypeStruct((2, CX, CY, CZ), f32),
            jax.ShapeDtypeStruct((2, NB), f32),
            jax.ShapeDtypeStruct((2, NB), f32),
        ),
        in_specs=[any_, any_, any_],
        out_specs=(hbm, hbm, hbm),
        scratch_shapes=[dma((3,))],
        compiler_params=pltpu.CompilerParams(vmem_limit_bytes=32 << 20),
        name="deliver",
    )(filtered, inter, proj)
    return filtered[:, None], inter, proj


def solution(mesh):
    return jax.shard_map(
        shards,
        mesh=mesh,
        in_specs=(P("band", "domain", None, None, None), P("domain", None, None, None)),
        out_specs=(P("band", "domain", None, None, None), P("band", None), P("band", None)),
        check_vma=False,
    )
```

```python
import functools

import jax
import jax.numpy as jnp
from jax import lax
from jax.experimental import pallas as pl
from jax.experimental.pallas import tpu as pltpu
from jax.sharding import PartitionSpec as P

second_coeffs = (
    -5369.0 / 1800.0,
    12.0 / 7.0,
    -15.0 / 56.0,
    10.0 / 189.0,
    -1.0 / 112.0,
    2.0 / 1925.0,
    -1.0 / 16632.0,
)
filter_center = 6.5
filter_half = 5.5
reach = 6
MESH = pl.DeviceIdType.MESH

CX, CY, CZ = 16, 16, 128
NY = 32
NB = 64
NCELL = 524288


def part_y(here):
    total = (-1.5 * second_coeffs[0]) * here
    for s in range(1, reach + 1):
        pair = pltpu.roll(here, s, 0) + pltpu.roll(here, NY - s, 0)
        total = total + (-0.5 * second_coeffs[s]) * pair
    return total


def part_z(here, beside, lane):
    total = None
    for s in range(1, reach + 1):
        ahead = pltpu.roll(jnp.where(lane < s, beside, here), CZ - s, 1)
        behind = pltpu.roll(jnp.where(lane >= CZ - s, beside, here), s, 1)
        term = (-0.5 * second_coeffs[s]) * (ahead + behind)
        total = term if total is None else total + term
    return total


def far_first(i, half):
    return half + ((i + 1) >> 1) * (2 * (i & 1) - 1)


def kernel(
    orb_in, pot_in, out_f, out_s, out_p,
    orb, give, pot, first, fil, zo, zf, zs, acc, hf, gf, gh, g_high, g_low, part, r1, r2, tot,
    loc_sem, in_send, in_recv, core_send, core_recv, x_send, x_recv,
    a2a_send, a2a_recv, back_send, back_recv, red_send, red_recv, ring,
):
    band = lax.axis_index("band")
    domain = lax.axis_index("domain")
    z, yh = band >> 2, band & 3
    x, yl, core = domain >> 2, (domain >> 1) & 1, domain & 1
    y = yh * 2 + yl
    zy = z * 8 + y
    mine = pl.multiple_of(yl * CY, CY)
    other = pl.multiple_of((1 - yl) * CY, CY)

    def at(pz, py, px, pc):
        return ((pz << 2) + (py >> 1), (px << 2) + ((py & 1) << 1) + pc)

    xn, xp = (x + 1) & 3, (x + 3) & 3
    yo = y + 1 - 2 * yl
    yq = (y + 7 + 2 * yl) & 7
    mate = at(z, y, x, 1 - core)
    to_xn, to_xp = at(z, y, xn, core), at(z, y, xp, core)

    def rdma(src, dst, send, recv, to):
        return pltpu.make_async_remote_copy(
            src_ref=src, dst_ref=dst, send_sem=send, recv_sem=recv,
            device_id=to, device_id_type=MESH,
        )

    mid = pl.ds(6, CX)
    low, high = pl.ds(0, 6), pl.ds(22, 6)
    rows = pl.ds(mine, CY)
    rows_other = pl.ds(other, CY)

    local = [
        pltpu.make_async_copy(orb_in.at[yl], orb.at[mid, rows], loc_sem.at[0]),
        pltpu.make_async_copy(orb_in.at[1 - yl], give, loc_sem.at[3]),
        pltpu.make_async_copy(pot_in, pot.at[:, rows], loc_sem.at[1]),
    ]
    for c in local:
        c.start()

    bar = pltpu.get_barrier_semaphore()
    up_z, down_z = at((z + 1) & 7, y, x, core), at((z + 7) & 7, y, x, core)
    up_y, down_y = at(z, (y + 1) & 7, x, core), at(z, (y + 7) & 7, x, core)
    for to in (up_y, down_y, to_xn, to_xp, up_z, down_z, mate):
        pl.semaphore_signal(bar, inc=1, device_id=to, device_id_type=MESH)
    pl.semaphore_wait(bar, 7)
    for c in local:
        c.wait()

    far_z = (at((z + 2) & 7, y, x, core), at((z + 6) & 7, y, x, core))
    far_y = (at(z, (y + 2) & 7, x, core), at(z, (y + 6) & 7, x, core))
    words = (
        (up_z, down_z), far_z, (up_y, down_y), (up_y, down_y), far_y, (mate,), (to_xn, to_xp), (to_xn, to_xp),
    )

    def tell(k):
        for to in words[k]:
            pl.semaphore_signal(ring.at[k], inc=1, device_id=to, device_id_type=MESH)

    def hear(k):
        pl.semaphore_wait(ring.at[k], len(words[k]))

    swaps = [
        rdma(
            give.at[pl.ds(k, n)], orb.at[pl.ds(k + 6, n), rows],
            in_send.at[i], in_recv.at[i], at(z, yo, x, core),
        )
        for i, (k, n) in enumerate(((0, 6), (10, 6), (6, 4)))
    ]
    direct = [
        rdma(orb.at[pl.ds(16, 6), rows], orb.at[low, rows], in_send.at[3], in_recv.at[3], to_xn),
        rdma(orb.at[pl.ds(6, 6), rows], orb.at[high, rows], in_send.at[4], in_recv.at[4], to_xp),
    ]
    given = rdma(pot.at[:, rows], pot.at[:, rows], in_send.at[5], in_recv.at[5], at(z, yq, x, core))

    def to_mate(k, src, dst):
        c = rdma(src, dst, core_send.at[k], core_recv.at[k], mate)
        c.start()
        return c

    for c in swaps[:2] + direct + [given]:
        c.start()
    beside = [to_mate(0, orb.at[mid, rows], zo.at[:, rows])]
    tell(0)

    lane = lax.broadcasted_iota(jnp.int32, (NY, CZ), 1)
    lane_half = lax.broadcasted_iota(jnp.int32, (CY, CZ), 1)

    def over_layers(body, first_layer=0, count=CX):
        def step(k, _):
            body(k)
            return 0

        lax.fori_loop(first_layer, first_layer + count, step, 0, unroll=2)

    def over_strips(src, first_layer, count, finish, base=0, strips=NY // 8):
        def strip(r, _):
            at_rows = pl.ds(pl.multiple_of(base + r * 8, 8), 8)
            line = [src[first_layer + j, at_rows] for j in range(count + 12)]
            for i in range(count):
                total = acc[first_layer + i, at_rows]
                for s in range(1, reach + 1):
                    total = total + (-0.5 * second_coeffs[s]) * (line[i + 6 + s] + line[i + 6 - s])
                finish(first_layer + i, at_rows, line[i + 6], total)
            return 0

        lax.fori_loop(0, strips, strip, 0, unroll=2)

    def along_y(src):
        def body(k):
            acc[k] = part_y(src[k + 6])

        return body

    def along_z(src, beside_src):
        def body(k):
            acc[k] = acc[k] + part_z(src[k + 6], beside_src[k], lane)

        return body

    def along_z_half(at_rows):
        def body(k):
            hf[k, at_rows] = part_z(orb[k + 6, at_rows], zo[k, at_rows], lane_half)

        return body

    def rim(src, k, to_next, at_rows=slice(None)):
        if to_next:
            c = rdma(src.at[pl.ds(16, 6), at_rows], src.at[low, at_rows], x_send.at[k], x_recv.at[k], to_xn)
        else:
            c = rdma(src.at[pl.ds(6, 6), at_rows], src.at[high, at_rows], x_send.at[k], x_recv.at[k], to_xp)
        c.start()
        return c

    beside[0].wait_recv()
    over_layers(along_z_half(rows))
    swaps[2].start()
    hear(0)
    tell(1)
    swaps[0].wait_recv()
    rims = [rim(orb, 0, False, rows_other)]
    swaps[1].wait_recv()
    rims.append(rim(orb, 1, True, rows_other))
    swaps[2].wait_recv()
    beside.append(to_mate(1, orb.at[mid, rows_other], zo.at[:, rows_other]))
    over_layers(along_y(orb))
    hear(1)
    tell(2)
    beside[1].wait_recv()
    over_layers(along_z_half(rows_other))
    given.wait_recv()

    def inner(src, finish):
        over_strips(src, 6, 4, finish)

    def edges(finish, before, arriving, src, k):
        sent = []
        for h, (base, at_rows) in enumerate(((mine, rows), (other, rows_other))):
            for c in arriving[h]:
                c.wait_recv()
            over_strips(before, 0, 6, finish, base, 2)
            sent.append([rim(src, k + 2 * h, False, at_rows)])
            over_strips(before, 10, 6, finish, base, 2)
            sent[h].append(rim(src, k + 2 * h + 1, True, at_rows))
        beside.append(to_mate(k // 4 + 2, src.at[mid], zf if k == 2 else zs))
        return sent

    def last_first(k, at_rows, here, total):
        h = total + hf[k, at_rows] + (pot[k, at_rows] - filter_center) * here
        first[k + 6, at_rows] = h * (1.0 / filter_half)

    inner(orb, last_first)
    rims_first = edges(last_first, orb, (direct, rims), first, 2)

    hear(2)
    tell(3)
    over_layers(along_y(first))
    hear(3)
    tell(4)
    beside[2].wait_recv()
    over_layers(along_z(first, zf))
    hear(4)
    tell(5)

    def layer_of(group, pz):
        m = pz >> 1
        return (6 + m, m, 4 + m + ((m >> 1) << 2), 12 + m)[group]

    def send_tiles(src, skip, got, which, pz, groups, at_home=False, parts=(0, 1)):
        for group in groups:
            for b in parts:
                py = (pz + group + 4 * b) & 7
                row = pl.multiple_of(16 * b + ((pz & 1) << 3), 8)
                copy = rdma(
                    src.at[skip + layer_of(group, pz), pl.ds(row, 8)], got.at[zy],
                    a2a_send.at[which], a2a_recv.at[which], at(pz, py, x, core),
                )
                if at_home:
                    pl.when(py != y)(copy.start)
                else:
                    copy.start()

    def all_tiles(got, which):
        return rdma(got.at[pl.ds(0, 63)], got.at[pl.ds(0, 63)], a2a_send.at[which], a2a_recv.at[which], mate)

    def send_all(src, skip, got, which, groups, parts=(0, 1), work=None):
        def turn(i, _):
            send_tiles(src, skip, got, which, (z + far_first(i, 4)) & 7, groups, False, parts)
            if work is not None:
                work(2 * i)
                work(2 * i + 1)
            return 0

        lax.fori_loop(0, 7, turn, 0)
        send_tiles(src, skip, got, which, z, groups, True, parts)
        if work is not None:
            work(14)
            work(15)

    def keep_tile(src, skip, got):
        group, b = (y + 8 - z) & 3, ((y + 8 - z) & 7) >> 2
        row = pl.multiple_of(16 * b + ((z & 1) << 3), 8)
        for k in range(4):
            @pl.when(group == k)
            def _():
                got[zy] = src[skip + layer_of(k, z), pl.ds(row, 8)]

    def last_filtered(k, at_rows, here, total):
        h = total + (pot[k, at_rows] - filter_center) * here
        fil[k + 6, at_rows] = h * (2.0 / filter_half) - orb[k + 6, at_rows]

    inner(first, last_filtered)
    send_all(fil, 6, gf, 0, (0,))
    rims_filtered = edges(last_filtered, first, rims_first, fil, 6)

    send_all(fil, 6, gf, 0, (1, 2, 3), work=along_y(fil))
    keep_tile(fil, 6, gf)
    hear(5)
    tell(6)

    def last_applied(k, at_rows, here, total):
        hf[k, at_rows] = total + pot[k, at_rows] * here

    beside[3].wait_recv()
    over_layers(along_z(fil, zs))
    hear(6)
    tell(7)
    inner(fil, last_applied)
    send_all(hf, 0, gh, 1, (0,))
    for h, base in enumerate((mine, other)):
        for c in rims_filtered[h]:
            c.wait_recv()
        over_strips(fil, 0, 6, last_applied, base, 2)
        over_strips(fil, 10, 6, last_applied, base, 2)
    send_all(hf, 0, gh, 1, (1, 2, 3))
    keep_tile(hf, 0, gh)

    def contract(left, right):
        return lax.dot_general(left, right, (((1,), (1,)), ((), ())), preferred_element_type=jnp.float32)

    def halves(value):
        upper = value.astype(jnp.bfloat16)
        return upper, (value - upper.astype(jnp.float32)).astype(jnp.bfloat16)

    def cells(got, s):
        return jnp.concatenate([got[:, 2 * s, :], got[:, 2 * s + 1, :]], axis=1)

    hear(7)
    all_tiles(gf, 0).wait_recv()
    over = jnp.zeros((NB, NB), jnp.float32)
    for s in range(4):
        upper, lower = halves(cells(gf, s))
        g_high[s] = upper
        g_low[s] = lower
        over = over + (contract(upper, upper) + (contract(upper, lower) + contract(lower, upper)))
    part[:, :, :NB] = over.reshape(32, 2, NB)
    all_tiles(gh, 1).wait_recv()
    proj = jnp.zeros((NB, NB), jnp.float32)
    for s in range(4):
        upper, lower = halves(cells(gh, s))
        proj = proj + (contract(g_high[s], upper) + (contract(g_high[s], lower) + contract(g_low[s], upper)))
    part[:, :, NB:] = proj.reshape(32, 2, NB)

    def send_rows(pz, at_home=False):
        for k in range(8):
            py = (y + far_first(k, 4)) & 7
            if not (at_home and k == 7):
                rdma(
                    part.at[(pz << 2) + (py >> 1)], r1.at[zy], red_send.at[0], red_recv.at[0], at(pz, py, x, core)
                ).start()

    def rows_out(i, _):
        send_rows((z + far_first(i, 4)) & 7)
        return 0

    lax.fori_loop(0, 7, rows_out, 0)
    send_rows(z, True)
    def give_back(k):
        c = rdma(
            fil.at[pl.ds(6 + 8 * k, 8), rows_other], out_f.at[yl, pl.ds(8 * k, 8)],
            back_send.at[k], back_recv.at[k], at(z, yo, x, core),
        )
        c.start()
        return c

    back = [give_back(0)]
    keep = pltpu.make_async_copy(fil.at[mid, rows], out_f.at[yl], loc_sem.at[2])
    keep.start()
    r1[zy] = part[band]
    red1 = rdma(r1.at[pl.ds(0, 63)], r1.at[pl.ds(0, 63)], red_send.at[0], red_recv.at[0], mate)
    red1.wait_recv()
    back.append(give_back(1))
    tot[...] = jnp.sum(r1[...], axis=0)
    slot = x * 2 + core
    for i in range(4):
        for pc in (1 - core, core)[: 2 if i < 3 else 1]:
            to = at(z, y, (x + far_first(i, 2)) & 3, pc)
            rdma(tot, r2.at[slot], red_send.at[1], red_recv.at[1], to).start()
    r2[slot] = tot[...]
    red2 = rdma(r2.at[pl.ds(0, 7)], r2.at[pl.ds(0, 7)], red_send.at[1], red_recv.at[1], mate)
    red2.wait_recv()
    result = jnp.sum(r2[...], axis=0) * (1.0 / NCELL)
    out_s[...] = result[:, :NB]
    out_p[...] = result[:, NB:]

    for c in swaps + direct + [given] + rims:
        c.wait_send()
    for c in beside:
        c.wait_send()
    for c in sum(rims_first, []):
        c.wait_send()
    for c in sum(rims_filtered, []):
        c.wait_send()
    all_tiles(gf, 0).wait_send()
    all_tiles(gh, 1).wait_send()
    red1.wait_send()
    red2.wait_send()
    keep.wait()
    for c in back:
        c.wait()


def deliver(filtered, inter, proj, out_f, out_s, out_p, sem):
    copies = [
        pltpu.make_async_copy(src, dst, sem.at[i])
        for i, (src, dst) in enumerate(((filtered, out_f), (inter, out_s), (proj, out_p)))
    ]
    for c in copies:
        c.start()
    for c in copies:
        c.wait()


def shards(orbitals, potential):
    f32 = jnp.float32
    vmem = pltpu.VMEM
    dma = pltpu.SemaphoreType.DMA
    any_ = pl.BlockSpec(memory_space=pl.ANY)
    hbm = pl.BlockSpec(memory_space=pltpu.HBM)
    full = pl.BlockSpec(memory_space=pltpu.VMEM)
    filtered, inter, proj = pl.pallas_call(
        kernel,
        out_shape=(
            jax.ShapeDtypeStruct((2, CX, CY, CZ), f32),
            jax.ShapeDtypeStruct((2, NB), f32),
            jax.ShapeDtypeStruct((2, NB), f32),
        ),
        in_specs=[hbm, hbm],
        out_specs=(hbm, full, full),
        scratch_shapes=[
            vmem((CX + 12, NY, CZ), f32),
            vmem((CX, CY, CZ), f32),
            vmem((CX, NY, CZ), f32),
            vmem((CX + 12, NY, CZ), f32),
            vmem((CX + 12, NY, CZ), f32),
            vmem((CX, NY, CZ), f32),
            vmem((CX, NY, CZ), f32),
            vmem((CX, NY, CZ), f32),
            vmem((CX, NY, CZ), f32),
            vmem((CX, NY, CZ), f32),
            vmem((NB, 8, CZ), f32),
            vmem((NB, 8, CZ), f32),
            vmem((4, NB, 2 * CZ), jnp.bfloat16),
            vmem((4, NB, 2 * CZ), jnp.bfloat16),
            vmem((32, 2, 2 * NB), f32),
            vmem((64, 2, 2 * NB), f32),
            vmem((8, 2, 2 * NB), f32),
            vmem((2, 2 * NB), f32),
            dma((4,)), dma((6,)), dma((6,)), dma((4,)), dma((4,)), dma((10,)), dma((10,)),
            dma((2,)), dma((2,)), dma((2,)), dma((2,)), dma((2,)), dma((2,)),
            pltpu.SemaphoreType.REGULAR((8,)),
        ],
        compiler_params=pltpu.CompilerParams(
            collective_id=0, has_side_effects=True, vmem_limit_bytes=32 << 20
        ),
        name="chebyshev_step",
    )(
        pltpu.with_memory_space_constraint(orbitals.reshape(2, CX, CY, CZ), pltpu.HBM),
        pltpu.with_memory_space_constraint(potential.reshape(CX, CY, CZ), pltpu.HBM),
    )
    filtered, inter, proj = pl.pallas_call(
        deliver,
        out_shape=(
            jax.ShapeDtypeStruct((2, CX, CY, CZ), f32),
            jax.ShapeDtypeStruct((2, NB), f32),
            jax.ShapeDtypeStruct((2, NB), f32),
        ),
        in_specs=[any_, any_, any_],
        out_specs=(hbm, hbm, hbm),
        scratch_shapes=[dma((3,))],
        compiler_params=pltpu.CompilerParams(vmem_limit_bytes=32 << 20),
        name="deliver",
    )(filtered, inter, proj)
    return filtered[:, None], inter, proj


def solution(mesh):
    return jax.shard_map(
        shards,
        mesh=mesh,
        in_specs=(P("band", "domain", None, None, None), P("domain", None, None, None)),
        out_specs=(P("band", "domain", None, None, None), P("band", None), P("band", None)),
        check_vma=False,
    )
```
